256 devices in a mesh: dp: 16 (over z, core), section: 4 (over x), mp: 4 (over y).
Axes of the slice: x: 4, y: 4, z: 8, core: 2. Of those that a mesh axis runs over, the one named last changes fastest.
Arguments:
- patches: bfloat16 [2, 1536, 1280], P(None, 'dp'), may hold values from -6 to 6
- image_sizes: int32 [2, 16, 4], P(None, 'dp'), may hold values from 1 to 18, as said below
- raster_order: int32 [2, 384], P(None, 'dp'), may hold values from 0 to 23, as said below
- image_starts: int32 [2, 16, 4], P(None, 'dp'), may hold values from 1 to 255, as said below
- qkv_weight: bfloat16 [4, 1280, 3840], P('section', 'dp', 'mp'), may hold values from -0.15625 to 0.15625
- proj_weight: bfloat16 [4, 1280, 1280], P('section', 'mp', 'dp'), may hold values from -0.15625 to 0.15625
- merge_in: bfloat16 [5120, 5120], P(None, ('section', 'mp')), may hold values from -0.078125 to 0.078125
- merge_out: bfloat16 [5120, 8192], P(('section', 'mp')), may hold values from -0.125 to 0.125
- text_embeds: bfloat16 [2, 4096, 8192], P(None, 'dp', ('section', 'mp')), may hold values from -6 to 6
- joined_grad: bfloat16 [2, 4096, 8192], P(None, 'dp', ('section', 'mp')), may hold values from -6 to 6
Outputs:
- joined: bfloat16 [2, 4096, 8192], P(None, 'dp', ('section', 'mp'))
- qkv_grad: float32 [4, 1280, 3840], P('section', 'dp', 'mp')
- proj_grad: float32 [4, 1280, 1280], P('section', 'mp', 'dp')
- merge_in_grad: float32 [5120, 5120], P('dp', ('section', 'mp'))
- merge_out_grad: float32 [5120, 8192], P(('section', 'mp'), 'dp')
The draws below stay inside these ranges and needn't reach their ends.
Inputs may be any that keep to these rules, and one draw needn't show every extreme that they name: `image_sizes`: for each micro-batch and data rank the 4 sizes sum to 24, and one of them is 18. `raster_order`: within each data rank's block of 24, a permutation that maps every image's span of places onto itself. `image_starts`: increasing within a rank's 4 images; the first is 1; each image's positions end at or before the next image's start; the last image's positions end at 256.
All inputs are finite; a program needn't handle non-finite values.
Results may differ from the reference program's by a relative error of at most 0.038.
Values may be sent and summed in bfloat16 or wider, within the bound.
No kernel may reach another device: no remote copies, remote signals or barrier semaphores. Data moves between devices by JAX's collectives and lax.ppermute only.
A program may use at most 128 MiB of HBM per device.

```python
import jax
import jax.numpy as jnp
from jax import lax

D_VIS = 1280
HEADS_VIS = 16
D_LLM = 8192
WINDOW = 16
IMGS = 4
MB = 2
MERGED_DEV = 24
SEQ_DEV = 256
D_MERGE = 5120
SECTIONS = 4
PATCHES = 1536
TOKENS = 4096
N_DP = 16


def drawn_sizes(key):
    key = jax.random.fold_in(key, 101)
    remain = MERGED_DEV // 4
    largest = MERGED_DEV - remain
    shape = (MB, N_DP)
    keys_list = jax.random.split(key, 3)
    first = jax.random.randint(keys_list[0], shape, 1, remain - 1)
    first = first.at[0, 0].set(1)
    second = jax.random.randint(keys_list[1], shape, jnp.ones(shape, jnp.int32), remain - first)
    third = remain - first - second
    table = jnp.stack([jnp.full(shape, largest, jnp.int32), first, second, third], axis=-1)
    turned = jax.random.randint(keys_list[2], shape + (1,), 0, 4)
    turned = turned.at[0, 0, 0].set(2)
    picks = (jnp.arange(4, dtype=jnp.int32)[None, None, :] + turned) % 4
    return jnp.take_along_axis(table, picks, axis=-1).astype(jnp.int32)


def draw_image_sizes(key, part):
    return drawn_sizes(key)


def draw_raster_order(key, part):
    image_sizes = drawn_sizes(key)
    key = jax.random.fold_in(key, 7)
    span_ends = jnp.cumsum(image_sizes, axis=-1, dtype=jnp.int32)
    places = jnp.arange(MERGED_DEV, dtype=jnp.int32)
    image_of = jnp.sum((places[None, None, :, None] >= span_ends[:, :, None, :]).astype(jnp.int32), axis=-1, dtype=jnp.int32)
    noise = jax.random.randint(key, image_of.shape, 0, 1024)
    scores = (image_of * 1024 + noise) * MERGED_DEV + places[None, None, :]
    order = jnp.argsort(scores, axis=-1, stable=True).astype(jnp.int32)
    return order.reshape(MB, N_DP * MERGED_DEV)


def draw_image_starts(key, part):
    image_sizes = drawn_sizes(key)
    key = jax.random.fold_in(key, 13)
    widest = (SEQ_DEV - MERGED_DEV) // IMGS
    gaps = jax.random.randint(key, (MB, N_DP, IMGS), 1, widest + 1)
    gaps = gaps.at[:, :, 0].set(1)
    starts = jnp.cumsum(gaps, axis=-1, dtype=jnp.int32) + jnp.cumsum(image_sizes, axis=-1, dtype=jnp.int32) - image_sizes
    last_start = SEQ_DEV - image_sizes[:, :, IMGS - 1]
    starts = starts.at[:, :, IMGS - 1].set(last_start)
    return starts.astype(jnp.int32)


def raised(result, rng, source, target, shards_of, factor):
    owner, partner = [(jnp.arange(result.shape[axis_at]) // (result.shape[axis_at] // shards_of)).reshape([-1 if axis == axis_at else 1 for axis in range(result.ndim)]) for axis_at in (source, target)]
    chosen = jax.random.permutation(rng, shards_of)[partner]
    strong = (owner == chosen) | (owner == (partner + shards_of // 2) % shards_of)
    return jnp.where(strong, factor * result, result)


def levels(key, dims, shards, low, high):
    gain, own = 1.0, jax.random.fold_in(key, 6)
    for position, shards_of in shards:
        draws = jnp.exp(jax.random.uniform(jax.random.fold_in(own, position), (shards_of,), jnp.float32, low / len(shards), high / len(shards)))
        gain = gain * jnp.repeat(draws, dims[position] // shards_of).reshape([-1 if axis == position else 1 for axis in range(len(dims))])
    return gain


def centred(own_key, extent, deviation, most, cuts=(), kind=jnp.bfloat16):
    drawn = jax.random.normal(own_key, extent, jnp.float32) * deviation
    if len(cuts) > 0:
        drawn = levels(own_key, extent, cuts, -0.22, 0.18) * drawn
    return jnp.clip(drawn, min=-most, max=most).astype(kind)


def heavy_noise(key, shape, scale, reach, cuts, heavy, held_as=jnp.bfloat16):
    result = scale * jax.random.normal(key, shape, jnp.float32)
    if cuts:
        result = result * levels(key, shape, cuts, -0.22, 0.18)
    return jnp.clip(raised(result, jax.random.fold_in(key, 3), *heavy), -reach, reach).astype(held_as)


def setup_inputs(seed: int = 0) -> dict:
    key_list = jax.random.split(jax.random.key(seed), 11)
    patches = centred(key_list[0], (MB, PATCHES, D_VIS), 1.0, 6.0, ((1, 16),))
    image_sizes = draw_image_sizes(jax.random.fold_in(key_list[10], 71), 0)
    raster_order = draw_raster_order(jax.random.fold_in(key_list[10], 71), 0)
    image_starts = draw_image_starts(jax.random.fold_in(key_list[10], 71), 0)
    qkv_weight = centred(key_list[4], (SECTIONS, D_VIS, 3 * D_VIS), D_VIS ** -0.5, 0.15625, ((0, 4), (1, 16), (2, 4)))
    proj_weight = centred(key_list[5], (SECTIONS, D_VIS, D_VIS), D_VIS ** -0.5, 0.15625, ((0, 4), (1, 4), (2, 16)))
    merge_in = centred(key_list[6], (D_MERGE, D_MERGE), D_MERGE ** -0.5, 0.078125, ((1, 16),))
    merge_out = heavy_noise(key_list[7], (D_MERGE, D_LLM), D_MERGE ** -0.5, 0.125, ((0, 16),), (0, 1, 16, 2.0))
    text_embeds = centred(key_list[8], (MB, TOKENS, D_LLM), 1.0, 6.0, ((1, 16), (2, 16)))
    joined_grad = centred(key_list[9], (MB, TOKENS, D_LLM), 1.0, 6.0, ((1, 16), (2, 16)))
    return dict(patches=patches, image_sizes=image_sizes, raster_order=raster_order, image_starts=image_starts, qkv_weight=qkv_weight, proj_weight=proj_weight, merge_in=merge_in, merge_out=merge_out, text_embeds=text_embeds, joined_grad=joined_grad)


EPSILON = 1e-06

def unit_rows(values):
    return values * lax.rsqrt(lax.optimization_barrier(jnp.mean(values * values, axis=-1, keepdims=True)) + EPSILON)

def image_layout(image_sizes, merged_rows, window):
    span_ends = jnp.cumsum(image_sizes, dtype=jnp.int32)
    span_starts = span_ends - image_sizes
    places = jnp.arange(merged_rows, dtype=jnp.int32)
    image_of = lax.optimization_barrier(jnp.sum((places[:, None] >= span_ends[None, :]).astype(jnp.int32), axis=1, dtype=jnp.int32))
    onehot = image_of[:, None] == jnp.arange(image_sizes.shape[0], dtype=jnp.int32)[None, :]
    offset = lax.optimization_barrier(jnp.sum(jnp.where(onehot, span_starts[None, :], 0), axis=1, dtype=jnp.int32))
    within = places - offset
    window_of = image_of * merged_rows + within // window
    return (image_of, within, window_of, onehot)

def patch_masks(image_sizes, merged_rows, window):
    image_of, within, window_of, onehot = image_layout(image_sizes, merged_rows, window)
    image_patch = jnp.repeat(image_of, 4)
    window_patch = jnp.repeat(window_of, 4)
    same_image = image_patch[:, None] == image_patch[None, :]
    same_window = window_patch[:, None] == window_patch[None, :]
    return (same_image, same_window)

def sequence_slots(image_sizes, image_starts, merged_rows, window):
    image_of, within, window_of, onehot = image_layout(image_sizes, merged_rows, window)
    return lax.optimization_barrier(jnp.sum(jnp.where(onehot, image_starts[None, :], 0), axis=1, dtype=jnp.int32)) + within

def attend(projected, key_mask, head_size):
    row_count = projected.shape[0]
    head_count = projected.shape[1] // (3 * head_size)
    pieces = projected.reshape(row_count, head_count, 3, head_size).astype(jnp.float32)
    queries = pieces[:, :, 0]
    keys_all = pieces[:, :, 1]
    values_all = pieces[:, :, 2]
    scores = jnp.einsum('thd,uhd->htu', queries, keys_all) * head_size ** (-0.5)
    scores = jnp.where(key_mask[None], scores, -1000000000.0)
    scores = scores - lax.optimization_barrier(jnp.max(scores, axis=-1, keepdims=True))
    weights = jnp.exp(scores)
    weights = (weights / lax.optimization_barrier(jnp.sum(weights, axis=-1, keepdims=True))).astype(jnp.bfloat16)
    mixed_heads = jnp.einsum('htu,uhd->thd', weights.astype(jnp.float32), values_all)
    return mixed_heads.reshape(row_count, head_count * head_size).astype(jnp.bfloat16)

def layer_inner(rows_in, joint_weight, key_mask, head_size):
    normed = unit_rows(rows_in.astype(jnp.float32)).astype(jnp.bfloat16)
    projected = jnp.dot(normed, joint_weight, preferred_element_type=jnp.float32).astype(jnp.bfloat16)
    mixed_heads = attend(projected, key_mask, head_size)
    return (normed, projected, mixed_heads)

def layer_back(rows_in, grad_out, joint_weight, out_weight, key_mask, head_size, add_heads):
    normed, projected, mixed_heads = layer_inner(rows_in, joint_weight, key_mask, head_size)
    grad_mixed = jnp.dot(grad_out, out_weight.T, preferred_element_type=jnp.float32).astype(jnp.bfloat16)
    grad_out_weight = jnp.dot(mixed_heads.T, grad_out, preferred_element_type=jnp.float32)
    unused, pull_back = jax.vjp(lambda values: attend(values, key_mask, head_size), projected)
    grad_projected = pull_back(grad_mixed)[0]
    grad_joint_weight = jnp.dot(normed.T, grad_projected, preferred_element_type=jnp.float32)
    grad_normed = add_heads(jnp.dot(grad_projected, joint_weight.T, preferred_element_type=jnp.float32))
    unused_norm, norm_back = jax.vjp(unit_rows, rows_in.astype(jnp.float32))
    grad_rows = (grad_out.astype(jnp.float32) + norm_back(grad_normed)[0]).astype(jnp.bfloat16)
    return (grad_rows, grad_joint_weight, grad_out_weight)

def exact_gelu(values):
    return jax.nn.gelu(values, approximate=False)

def rank_pass(patch_rank, sizes_rank, order_rank, starts_rank, text_rank, grad_rank, qkv_weight, proj_weight, merge_in, merge_out):
    micro_count, patch_rows, width = patch_rank.shape
    merged_rows = patch_rows // 4
    head_size = width // HEADS_VIS
    mask_pairs = [patch_masks(sizes_rank[micro_index], merged_rows, WINDOW) for micro_index in range(micro_count)]
    layer_inputs = []
    finals = []
    for micro_index in range(micro_count):
        rows_now = patch_rank[micro_index]
        kept = []
        for layer in range(SECTIONS):
            key_mask = mask_pairs[micro_index][0] if layer == SECTIONS - 1 else mask_pairs[micro_index][1]
            kept.append(rows_now)
            normed, projected, mixed_heads = layer_inner(rows_now, qkv_weight[layer], key_mask, head_size)
            summed = jnp.dot(mixed_heads, proj_weight[layer], preferred_element_type=jnp.float32)
            rows_now = (rows_now.astype(jnp.float32) + summed).astype(jnp.bfloat16)
        layer_inputs.append(kept)
        finals.append(rows_now)
    flat_rows = jnp.stack(finals).astype(jnp.float32)
    merged_input = unit_rows(flat_rows).astype(jnp.bfloat16).reshape(micro_count * merged_rows, 4 * width)
    before_act = jnp.dot(merged_input, merge_in, preferred_element_type=jnp.float32)
    activated = exact_gelu(before_act).astype(jnp.bfloat16)
    visual = jnp.dot(activated, merge_out, preferred_element_type=jnp.float32).astype(jnp.bfloat16)
    visual = visual.reshape(micro_count, merged_rows, visual.shape[-1])
    joined_list = []
    grad_list = []
    for micro_index in range(micro_count):
        slots = sequence_slots(sizes_rank[micro_index], starts_rank[micro_index], merged_rows, WINDOW)
        raster = order_rank[micro_index]
        placed = visual[micro_index][raster]
        joined_list.append(text_rank[micro_index].at[slots].set(placed))
        grad_raster = grad_rank[micro_index][slots]
        grad_list.append(jnp.zeros_like(placed).at[raster].set(grad_raster))
    visual_grad = jnp.stack(grad_list).reshape(micro_count * merged_rows, -1)
    grad_activated = jnp.dot(visual_grad, merge_out.T, preferred_element_type=jnp.float32)
    unused, gelu_back = jax.vjp(exact_gelu, before_act)
    grad_before = gelu_back(grad_activated)[0].astype(jnp.bfloat16)
    grad_merged = jnp.dot(grad_before, merge_in.T, preferred_element_type=jnp.float32)
    unused_norm, norm_back = jax.vjp(unit_rows, flat_rows)
    final_grads = norm_back(grad_merged.reshape(flat_rows.shape))[0].astype(jnp.bfloat16)
    merge_in_part = jnp.dot(merged_input.T, grad_before, preferred_element_type=jnp.float32)
    merge_out_part = jnp.dot(activated.T, visual_grad, preferred_element_type=jnp.float32)
    qkv_parts = [jnp.zeros(qkv_weight.shape[1:], jnp.float32) for layer in range(SECTIONS)]
    proj_parts = [jnp.zeros(proj_weight.shape[1:], jnp.float32) for layer in range(SECTIONS)]
    for micro_index in range(micro_count):
        grad_now = final_grads[micro_index]
        for layer in range(SECTIONS - 1, -1, -1):
            key_mask = mask_pairs[micro_index][0] if layer == SECTIONS - 1 else mask_pairs[micro_index][1]
            grad_now, grad_joint, grad_outw = layer_back(layer_inputs[micro_index][layer], grad_now, qkv_weight[layer], proj_weight[layer], key_mask, head_size, lambda values: values)
            qkv_parts[layer] = qkv_parts[layer] + grad_joint
            proj_parts[layer] = proj_parts[layer] + grad_outw
    return (jnp.stack(joined_list), (jnp.stack(qkv_parts), jnp.stack(proj_parts), merge_in_part, merge_out_part))

def reference(patches, image_sizes, raster_order, image_starts, qkv_weight, proj_weight, merge_in, merge_out, text_embeds, joined_grad):

    def split_ranks(array):
        shaped = array.reshape((array.shape[0], N_DP, array.shape[1] // N_DP) + array.shape[2:])
        return jnp.swapaxes(shaped, 0, 1)
    inputs = (split_ranks(patches), jnp.swapaxes(image_sizes, 0, 1), split_ranks(raster_order), jnp.swapaxes(image_starts, 0, 1), split_ranks(text_embeds), split_ranks(joined_grad))
    initial = (jnp.zeros(qkv_weight.shape, jnp.float32), jnp.zeros(proj_weight.shape, jnp.float32), jnp.zeros(merge_in.shape, jnp.float32), jnp.zeros(merge_out.shape, jnp.float32))

    def one_rank(totals, rank_inputs):
        joined_rank, partials = rank_pass(*rank_inputs, qkv_weight, proj_weight, merge_in, merge_out)
        totals = tuple((total + lax.optimization_barrier(piece.astype(jnp.bfloat16)).astype(jnp.float32) for total, piece in zip(totals, partials)))
        return (totals, joined_rank)
    totals, joined_ranks = lax.scan(one_rank, initial, inputs)
    joined = jnp.swapaxes(joined_ranks, 0, 1).reshape(text_embeds.shape)
    return (joined, totals[0], totals[1], totals[2], totals[3])
```

```python
import functools
import math

import jax
import jax.numpy as jnp
from jax import lax
from jax.experimental import pallas as pl
from jax.experimental.pallas import tpu as pltpu
from jax.sharding import PartitionSpec as P

HEADS_VIS = 16
WINDOW = 16
EPSILON = 1e-06

QUARTERS = 4
SECTIONS = 4
HEADS = HEADS_VIS // QUARTERS
HEAD = 80
WIDTH = 1280
MERGED = 24
TOKENS = 2 * MERGED
ROWS = QUARTERS * TOKENS
QKV = 3 * HEADS * HEAD
MIX = HEADS * HEAD
PROJ_AT = 1024
JOINT = PROJ_AT + MIX
HIDDEN = 320
FEATURES = 512
SCALE = HEAD ** (-0.5)

bf16 = jnp.bfloat16
f32 = jnp.float32


def permute(value, pairs):
    return lax.ppermute(value, ("section", "mp"), pairs)


def around(section, steps):
    return [
        (QUARTERS * section + m, QUARTERS * section + (m + steps) % QUARTERS)
        for m in range(QUARTERS)
    ]


def around_all(steps):
    return [pair for section in range(SECTIONS) for pair in around(section, steps)]


def across(source, target):
    return [(QUARTERS * source + m, QUARTERS * target + m) for m in range(QUARTERS)]


def dot(a, b):
    return lax.dot_general(a, b, (((1,), (0,)), ((), ())), preferred_element_type=f32)


def dot_nt(a, b):
    return lax.dot_general(a, b, (((1,), (1,)), ((), ())), preferred_element_type=f32)


def dot_tn(a, b):
    return lax.dot_general(a, b, (((0,), (0,)), ((), ())), preferred_element_type=f32)


def unit_rows(values):
    return values * lax.rsqrt(jnp.mean(values * values, axis=-1, keepdims=True) + EPSILON)


def unit_back(values, cotangent):
    inverse = lax.rsqrt(jnp.mean(values * values, axis=-1, keepdims=True) + EPSILON)
    along = jnp.mean(cotangent * values, axis=-1, keepdims=True)
    return inverse * cotangent - values * (inverse * inverse * inverse * along)


def image_layout(image_sizes):
    span_ends = jnp.cumsum(image_sizes, dtype=jnp.int32)
    span_starts = span_ends - image_sizes
    places = jnp.arange(MERGED, dtype=jnp.int32)
    image_of = jnp.sum(
        (places[:, None] >= span_ends[None, :]).astype(jnp.int32), axis=1, dtype=jnp.int32
    )
    onehot = image_of[:, None] == jnp.arange(image_sizes.shape[0], dtype=jnp.int32)[None, :]
    offset = jnp.sum(jnp.where(onehot, span_starts[None, :], 0), axis=1, dtype=jnp.int32)
    return (image_of, places - offset, onehot)


def block_rows(place, step):
    return pl.ds(pl.multiple_of(lax.rem(place + step + QUARTERS, QUARTERS) * TOKENS, 16), TOKENS)


def gather_blocks(place, blocks, held):
    for step in range(QUARTERS):
        held[block_rows(place, -step), :] = blocks[step][...]


def head_parts(projected, head):
    at = 3 * HEAD * head
    return (
        projected[:, at : at + HEAD],
        projected[:, at + HEAD : at + 2 * HEAD],
        projected[:, at + 2 * HEAD : at + 3 * HEAD],
    )


def head_weights(queries, keys, same):
    scores = jnp.where(same, dot_nt(queries, keys) * SCALE, -1000000000.0)
    raised = jnp.exp(scores - jnp.max(scores, axis=-1, keepdims=True))
    return raised / jnp.sum(raised, axis=-1, keepdims=True)


def inner_rows(held, weight, same):
    normed = unit_rows(held[...].astype(f32)).astype(bf16)
    projected = dot(normed, weight[:, :QKV]).astype(bf16)
    mixed = []
    for head in range(HEADS):
        queries, keys, values = head_parts(projected, head)
        mixed.append(dot(head_weights(queries, keys, same).astype(bf16), values).astype(bf16))
    return normed, projected, jnp.concatenate(mixed, axis=1)


def send_blocks(place, whole, outs):
    for step in range(QUARTERS):
        outs[step][...] = whole[block_rows(place, step), :].astype(outs[step].dtype)


def forward_kernel(place_ref, down, across_ref, x0, x1, x2, x3, weight, o0, o1, o2, o3, held, part):
    place = place_ref[0]
    gather_blocks(place, (x0, x1, x2, x3), held)
    same = down[...] == across_ref[...]
    _, _, mixed = inner_rows(held, weight, same)
    part[...] = dot_nt(mixed, weight[:, PROJ_AT:])
    send_blocks(place, part, (o0, o1, o2, o3))


def keep_kernel(place_ref, down, across_ref, x0, x1, x2, x3, weight, normed, projected, mixed, held):
    gather_blocks(place_ref[0], (x0, x1, x2, x3), held)
    same = down[...] == across_ref[...]
    normed[...], projected[...], mixed[...] = inner_rows(held, weight, same)


def grad_heads(grad_out, projected, weight, same):
    grad_mixed = dot(grad_out, weight[:, PROJ_AT:]).astype(bf16)
    pieces = []
    for head in range(HEADS):
        queries, keys, values = head_parts(projected, head)
        weights = head_weights(queries, keys, same)
        grad_head = grad_mixed[:, HEAD * head : HEAD * (head + 1)]
        grad_values = dot_tn(weights.astype(bf16), grad_head)
        grad_weights = dot_nt(grad_head, values).astype(bf16).astype(f32)
        centre = jnp.sum(grad_weights * weights, axis=-1, keepdims=True)
        grad_scores = (weights * (grad_weights - centre) * SCALE).astype(bf16)
        pieces += [dot(grad_scores, keys), dot_tn(grad_scores, queries), grad_values]
    return jnp.concatenate([piece.astype(bf16) for piece in pieces], axis=1)


def backward_kernel(
    place_ref,
    down,
    across_ref,
    g0,
    g1,
    g2,
    g3,
    projected,
    weight,
    g_before,
    p_before,
    g_after,
    p_after,
    o0,
    o1,
    o2,
    o3,
    held,
    part,
):
    place = place_ref[0]
    gather_blocks(place, (g0, g1, g2, g3), held)
    same = down[...] == across_ref[...]
    grad_out = held[...]
    grad_projected = grad_heads(grad_out, projected[...], weight, same)
    part[...] = dot_nt(grad_projected, weight[:, :QKV])
    send_blocks(place, part, (o0, o1, o2, o3))
    g_after[...] = g_before[...] + grad_out
    p_after[...] = p_before[...] + grad_projected


def last_kernel(
    place_ref,
    down,
    across_ref,
    g0,
    g1,
    g2,
    g3,
    projected,
    weight,
    g_before,
    p_before,
    normed,
    mixed,
    joint_grad,
    held,
):
    gather_blocks(place_ref[0], (g0, g1, g2, g3), held)
    same = down[...] == across_ref[...]
    grad_projected = p_before[...] + grad_heads(held[...], projected[...], weight, same)
    step = WIDTH // 5
    for at in range(0, WIDTH, step):
        rows = slice(at, at + step)
        joint_grad[rows, :QKV] = dot_tn(normed[:, rows], grad_projected).astype(bf16)
        joint_grad[rows, QKV:PROJ_AT] = jnp.zeros((step, PROJ_AT - QKV), bf16)
        grad_rows = g_before[:, rows] + held[:, rows]
        joint_grad[rows, PROJ_AT:] = dot_tn(grad_rows, mixed[...]).astype(bf16)


def merge_kernel(
    place_ref, x0, x1, x2, x3, weight, grad_act, merged, activated, grad_before, o0, o1, o2, o3, held
):
    place = place_ref[0]
    blocks = (x0, x1, x2, x3)
    before = jnp.zeros((TOKENS, HIDDEN), f32)
    for step in range(QUARTERS):
        owner = lax.rem(place - step + QUARTERS, QUARTERS)
        normed = unit_rows(blocks[step][...].astype(f32)).astype(bf16)
        held[owner] = normed
        rows = pl.ds(pl.multiple_of(owner * WIDTH, WIDTH), WIDTH)
        before = before + dot(normed, weight[rows, :])
    for quarter in range(QUARTERS):
        merged[:, quarter * WIDTH : (quarter + 1) * WIDTH] = held[quarter]
    tail = 0.5 * (1.0 + lax.erf(before * math.sqrt(0.5)))
    bell = jnp.exp(-0.5 * before * before) * (1.0 / math.sqrt(2.0 * math.pi))
    activated[...] = (before * tail).astype(bf16)
    grad = ((tail + before * bell) * grad_act[...]).astype(bf16)
    grad_before[...] = grad
    outs = (o0, o1, o2, o3)
    for step in range(QUARTERS):
        owner = lax.rem(place + step, QUARTERS)
        rows = pl.ds(pl.multiple_of(owner * WIDTH, WIDTH), WIDTH)
        outs[step][...] = dot_nt(grad, weight[rows, :]).astype(outs[step].dtype)


def call(kernel, operands, results, scratch, flops, moved):
    return pl.pallas_call(
        kernel,
        in_specs=[pl.BlockSpec(memory_space=pltpu.SMEM)]
        + [pl.BlockSpec(memory_space=pltpu.VMEM)] * (len(operands) - 1),
        out_specs=[pl.BlockSpec(memory_space=pltpu.VMEM)] * len(results),
        out_shape=[jax.ShapeDtypeStruct(shape, kind) for shape, kind in results],
        scratch_shapes=[pltpu.VMEM(shape, kind) for shape, kind in scratch],
        compiler_params=pltpu.CompilerParams(vmem_limit_bytes=40 * 1024 * 1024),
        cost_estimate=pl.CostEstimate(flops=flops, bytes_accessed=moved, transcendentals=0),
    )(*operands)


BLOCK = (TOKENS, WIDTH)
PARTS = [(BLOCK, f32)] + [(BLOCK, bf16)] * 3


def local(
    patches,
    image_sizes,
    raster_order,
    image_starts,
    qkv_weight,
    proj_weight,
    merge_in,
    merge_out,
    text_embeds,
    joined_grad,
):
    section = lax.axis_index("section")
    place = lax.axis_index("mp")
    place_ref = place.reshape(1)
    is_last = section == SECTIONS - 1

    joint_local = jnp.concatenate(
        [qkv_weight[0], jnp.zeros((WIDTH // 16, PROJ_AT - QKV), bf16), proj_weight[0].T], axis=1
    )
    joint = lax.all_gather(joint_local, "dp", axis=0, tiled=True)

    marks = []
    spots = []
    for micro in range(2):
        image_of, within, onehot = image_layout(image_sizes[micro, 0])
        window_of = image_of * MERGED + within // WINDOW
        marks.append(jnp.where(is_last, image_of, window_of) + micro * 1024)
        starts = jnp.where(onehot, image_starts[micro, 0][None, :], 0)
        slots = jnp.sum(starts, axis=1, dtype=jnp.int32) + within
        order = raster_order[micro]
        from_raster = order[None, :] == jnp.arange(MERGED, dtype=jnp.int32)[:, None]
        spots.append(jnp.sum(jnp.where(from_raster, slots[None, :], 0), axis=1, dtype=jnp.int32))
    mark = jnp.tile(jnp.concatenate(marks), QUARTERS)
    down, right = mark[:, None], mark[None, :]
    positions = jnp.arange(text_embeds.shape[1], dtype=jnp.int32)
    chosen = jnp.stack(spots)[:, :, None] == positions[None, None, :]
    chosen_bf = chosen.astype(bf16)

    visual_grad = jnp.einsum(
        "mts,msf->mtf", chosen_bf, joined_grad, preferred_element_type=f32
    ).astype(bf16)
    visual_grad = visual_grad.reshape(TOKENS, FEATURES)
    visual_grad_full = lax.all_gather(visual_grad, ("section", "mp"), axis=1, tiled=True)
    grad_act = jnp.dot(visual_grad_full, merge_out.T, preferred_element_type=f32)

    quarters = jnp.swapaxes(patches.reshape(TOKENS, QUARTERS, WIDTH), 0, 1)
    blocks = [
        lax.dynamic_index_in_dim(quarters, (place + QUARTERS - step) % QUARTERS, 0, False)
        for step in range(QUARTERS)
    ]
    first = section == 0
    saved = [jnp.where(first, block, jnp.zeros_like(block)) for block in blocks]

    layer_flops = 2 * ROWS * WIDTH * JOINT
    layer_bytes = 2 * WIDTH * JOINT + 8 * ROWS * WIDTH
    held = ((ROWS, WIDTH), bf16)
    part = ((ROWS, WIDTH), f32)
    final = None
    for stage in range(SECTIONS):
        terms = call(
            forward_kernel,
            [place_ref, down, right, *blocks, joint],
            PARTS,
            [held, part],
            layer_flops,
            layer_bytes,
        )
        total = blocks[0].astype(f32) + terms[0]
        for step in range(1, QUARTERS):
            total = total + permute(terms[step], around(stage, step)).astype(f32)
        leaving = total.astype(bf16)
        if stage == SECTIONS - 1:
            final = leaving
            break
        entered = permute(leaving, across(stage, stage + 1))
        blocks = [entered] + [
            permute(entered, around(stage + 1, step)) for step in range(1, QUARTERS)
        ]
        saved = [old + new for old, new in zip(saved, blocks)]

    sent = [permute(final, across(SECTIONS - 1, target)) for target in range(SECTIONS - 1)]
    own = jnp.where(is_last, final, sent[0] + sent[1] + sent[2])
    final_blocks = [own] + [permute(own, around_all(step)) for step in range(1, QUARTERS)]
    merged, activated, grad_before, *terms = call(
        merge_kernel,
        [place_ref, *final_blocks, merge_in, grad_act],
        [
            ((TOKENS, QUARTERS * WIDTH), bf16),
            ((TOKENS, HIDDEN), bf16),
            ((TOKENS, HIDDEN), bf16),
        ]
        + PARTS,
        [((QUARTERS, TOKENS, WIDTH), bf16)],
        4 * TOKENS * QUARTERS * WIDTH * HIDDEN,
        2 * QUARTERS * WIDTH * HIDDEN,
    )
    normed, projected, mixed = call(
        keep_kernel,
        [place_ref, down, right, *saved, joint],
        [((ROWS, WIDTH), bf16), ((ROWS, QKV), bf16), ((ROWS, MIX), bf16)],
        [held],
        layer_flops,
        layer_bytes,
    )

    total = terms[0]
    for step in range(1, QUARTERS):
        total = total + permute(terms[step], around_all(step)).astype(f32)
    leaving = total.astype(bf16)
    for source in range(SECTIONS - 1):
        total = total + permute(leaving, across(source, SECTIONS - 1)).astype(f32)
    grad_own = unit_back(own.astype(f32), total)
    grad_own = jnp.where(is_last, grad_own, 0.0).astype(bf16)

    whole_in = lax.dot_general(
        merged, grad_before, (((0,), (0,)), ((), ())), preferred_element_type=f32
    ).astype(bf16)
    merge_in_grad = lax.psum_scatter(whole_in, "dp", scatter_dimension=0, tiled=True).astype(f32)
    whole_out = jnp.einsum(
        "tr,tjc->jrc",
        activated,
        visual_grad_full.reshape(TOKENS, 16, FEATURES),
        preferred_element_type=f32,
    ).astype(bf16)
    merge_out_grad = lax.psum_scatter(
        whole_out, "dp", scatter_dimension=0, tiled=False
    ).astype(f32)

    visual_terms = jnp.dot(activated, merge_out, preferred_element_type=f32)
    visual_terms = visual_terms.reshape(TOKENS, SECTIONS, QUARTERS * FEATURES)
    take = lambda array, at: lax.dynamic_index_in_dim(array, at, 1, False)
    visual = take(visual_terms, section)
    for step in range(1, SECTIONS):
        term = take(visual_terms, (section + step) % SECTIONS).astype(bf16)
        pairs = [(s, (s + step) % SECTIONS) for s in range(SECTIONS)]
        visual = visual + lax.ppermute(term, "section", pairs).astype(f32)
    visual_terms = visual.reshape(TOKENS, QUARTERS, FEATURES)
    visual = take(visual_terms, place)
    for step in range(1, QUARTERS):
        term = take(visual_terms, (place + step) % QUARTERS).astype(bf16)
        pairs = [(m, (m + step) % QUARTERS) for m in range(QUARTERS)]
        visual = visual + lax.ppermute(term, "mp", pairs).astype(f32)
    visual = visual.astype(bf16).reshape(2, MERGED, FEATURES)
    placed = jnp.einsum("mts,mtf->msf", chosen_bf, visual, preferred_element_type=f32)
    taken = jnp.any(chosen, axis=1)[:, :, None]
    joined = jnp.where(taken, placed.astype(bf16), text_embeds)

    grad_rows = jnp.zeros((ROWS, WIDTH), bf16)
    grad_projected = jnp.zeros((ROWS, QKV), bf16)
    for layer in range(SECTIONS - 1, -1, -1):
        grads = [grad_own] + [permute(grad_own, around(layer, step)) for step in range(1, QUARTERS)]
        operands = [place_ref, down, right, *grads, projected, joint, grad_rows, grad_projected]
        if layer == 0:
            break
        grad_rows, grad_projected, *terms = call(
            backward_kernel,
            operands,
            [((ROWS, WIDTH), bf16), ((ROWS, QKV), bf16)] + PARTS,
            [held, part],
            layer_flops,
            layer_bytes,
        )
        total = terms[0]
        for step in range(1, QUARTERS):
            total = total + permute(terms[step], around(layer, step)).astype(f32)
        grad_next = grad_own.astype(f32) + unit_back(saved[0].astype(f32), total)
        grad_own = permute(grad_next.astype(bf16), across(layer, layer - 1))
    (joint_grad,) = call(
        last_kernel,
        [*operands, normed, mixed],
        [((WIDTH, JOINT), bf16)],
        [held],
        2 * layer_flops,
        2 * layer_bytes,
    )
    reduced = lax.psum_scatter(joint_grad, "dp", scatter_dimension=0, tiled=True)
    qkv_grad = reduced[:, :QKV].astype(f32)
    proj_grad = reduced[:, PROJ_AT:].T.astype(f32)
    return (joined, qkv_grad[None], proj_grad[None], merge_in_grad, merge_out_grad)


def solution(mesh):
    return jax.shard_map(
        local,
        mesh=mesh,
        in_specs=(
            P(None, "dp", None),
            P(None, "dp", None),
            P(None, "dp"),
            P(None, "dp", None),
            P("section", "dp", "mp"),
            P("section", "mp", "dp"),
            P(None, ("section", "mp")),
            P(("section", "mp"), None),
            P(None, "dp", ("section", "mp")),
            P(None, "dp", ("section", "mp")),
        ),
        out_specs=(
            P(None, "dp", ("section", "mp")),
            P("section", "dp", "mp"),
            P("section", "mp", "dp"),
            P("dp", ("section", "mp")),
            P(("section", "mp"), "dp"),
        ),
        check_vma=False,
    )
```

```python
import functools
import math

import jax
import jax.numpy as jnp
from jax import lax
from jax.experimental import pallas as pl
from jax.experimental.pallas import tpu as pltpu
from jax.sharding import PartitionSpec as P

HEADS_VIS = 16
WINDOW = 16
EPSILON = 1e-06

QUARTERS = 4
SECTIONS = 4
HEADS = HEADS_VIS // QUARTERS
HEAD = 80
WIDTH = 1280
MERGED = 24
TOKENS = 2 * MERGED
ROWS = QUARTERS * TOKENS
QKV = 3 * HEADS * HEAD
MIX = HEADS * HEAD
PROJ_AT = 1024
JOINT = PROJ_AT + MIX
HIDDEN = 320
FEATURES = 512
SCALE = HEAD ** (-0.5)

bf16 = jnp.bfloat16
f32 = jnp.float32


def permute(value, pairs):
    return lax.ppermute(value, ("section", "mp"), pairs)


def across(source, target, steps=0):
    return [
        (QUARTERS * source + m, QUARTERS * target + (m + steps) % QUARTERS)
        for m in range(QUARTERS)
    ]


def to_section(value, source, target):
    return [permute(value, across(source, target, step)) for step in range(QUARTERS)]


def exchange(value):
    return lax.all_to_all(value, "mp", 0, 0)


def everyones(value):
    return exchange(jnp.broadcast_to(value[None], (QUARTERS, *value.shape)))


def dot(a, b):
    return lax.dot_general(a, b, (((1,), (0,)), ((), ())), preferred_element_type=f32)


def dot_nt(a, b):
    return lax.dot_general(a, b, (((1,), (1,)), ((), ())), preferred_element_type=f32)


def dot_tn(a, b):
    return lax.dot_general(a, b, (((0,), (0,)), ((), ())), preferred_element_type=f32)


def unit_rows(values):
    return values * lax.rsqrt(jnp.mean(values * values, axis=-1, keepdims=True) + EPSILON)


def unit_back(values, cotangent):
    inverse = lax.rsqrt(jnp.mean(values * values, axis=-1, keepdims=True) + EPSILON)
    along = jnp.mean(cotangent * values, axis=-1, keepdims=True)
    return inverse * cotangent - values * (inverse * inverse * inverse * along)


def image_layout(image_sizes):
    span_ends = jnp.cumsum(image_sizes, dtype=jnp.int32)
    span_starts = span_ends - image_sizes
    places = jnp.arange(MERGED, dtype=jnp.int32)
    image_of = jnp.sum(
        (places[:, None] >= span_ends[None, :]).astype(jnp.int32), axis=1, dtype=jnp.int32
    )
    onehot = image_of[:, None] == jnp.arange(image_sizes.shape[0], dtype=jnp.int32)[None, :]
    offset = jnp.sum(jnp.where(onehot, span_starts[None, :], 0), axis=1, dtype=jnp.int32)
    return (image_of, places - offset, onehot)


def gather_blocks(place_ref, blocks, held, turned):
    for step in range(QUARTERS):
        if turned:
            owner = lax.rem(place_ref[0] - step + QUARTERS, QUARTERS)
            rows = pl.ds(pl.multiple_of(owner * TOKENS, 16), TOKENS)
        else:
            rows = slice(step * TOKENS, (step + 1) * TOKENS)
        held[rows, :] = blocks[step][...]


def head_parts(projected, head):
    at = 3 * HEAD * head
    return (
        projected[:, at : at + HEAD],
        projected[:, at + HEAD : at + 2 * HEAD],
        projected[:, at + 2 * HEAD : at + 3 * HEAD],
    )


def head_weights(queries, keys, same):
    scores = jnp.where(same, dot_nt(queries, keys) * SCALE, -1000000000.0)
    raised = jnp.exp(scores - jnp.max(scores, axis=-1, keepdims=True))
    return raised / jnp.sum(raised, axis=-1, keepdims=True)


def inner_rows(held, weight, same):
    normed = unit_rows(held[...].astype(f32)).astype(bf16)
    projected = dot(normed, weight[:, :QKV]).astype(bf16)
    mixed = []
    for head in range(HEADS):
        queries, keys, values = head_parts(projected, head)
        mixed.append(dot(head_weights(queries, keys, same).astype(bf16), values).astype(bf16))
    return normed, projected, jnp.concatenate(mixed, axis=1)


def forward_kernel(place_ref, down, across_ref, x0, x1, x2, x3, weight, part, held, *, turned):
    gather_blocks(place_ref, (x0, x1, x2, x3), held, turned)
    same = down[...] == across_ref[...]
    _, _, mixed = inner_rows(held, weight, same)
    total = dot_nt(mixed, weight[:, PROJ_AT:]).astype(bf16)
    for quarter in range(QUARTERS):
        part[quarter] = total[quarter * TOKENS : (quarter + 1) * TOKENS]


def keep_kernel(place_ref, down, across_ref, x0, x1, x2, x3, weight, normed, projected, mixed, held):
    gather_blocks(place_ref, (x0, x1, x2, x3), held, True)
    same = down[...] == across_ref[...]
    normed[...], projected[...], mixed[...] = inner_rows(held, weight, same)


def grad_heads(grad_out, projected, weight, same):
    grad_mixed = dot(grad_out, weight[:, PROJ_AT:]).astype(bf16)
    pieces = []
    for head in range(HEADS):
        queries, keys, values = head_parts(projected, head)
        weights = head_weights(queries, keys, same)
        grad_head = grad_mixed[:, HEAD * head : HEAD * (head + 1)]
        grad_values = dot_tn(weights.astype(bf16), grad_head)
        grad_weights = dot_nt(grad_head, values).astype(bf16).astype(f32)
        centre = jnp.sum(grad_weights * weights, axis=-1, keepdims=True)
        grad_scores = (weights * (grad_weights - centre) * SCALE).astype(bf16)
        pieces += [dot(grad_scores, keys), dot_tn(grad_scores, queries), grad_values]
    return jnp.concatenate([piece.astype(bf16) for piece in pieces], axis=1)


def backward_kernel(
    place_ref,
    down,
    across_ref,
    g0,
    g1,
    g2,
    g3,
    projected,
    weight,
    g_before,
    p_before,
    g_after,
    p_after,
    part,
    held,
    *,
    turned,
):
    gather_blocks(place_ref, (g0, g1, g2, g3), held, turned)
    same = down[...] == across_ref[...]
    grad_out = held[...]
    grad_projected = grad_heads(grad_out, projected[...], weight, same)
    total = dot_nt(grad_projected, weight[:, :QKV]).astype(bf16)
    for quarter in range(QUARTERS):
        part[quarter] = total[quarter * TOKENS : (quarter + 1) * TOKENS]
    g_after[...] = g_before[...] + grad_out
    p_after[...] = p_before[...] + grad_projected


def last_kernel(
    place_ref,
    down,
    across_ref,
    g0,
    g1,
    g2,
    g3,
    projected,
    weight,
    g_before,
    p_before,
    normed,
    mixed,
    joint_grad,
    held,
):
    gather_blocks(place_ref, (g0, g1, g2, g3), held, True)
    same = down[...] == across_ref[...]
    grad_projected = p_before[...] + grad_heads(held[...], projected[...], weight, same)
    step = WIDTH // 5
    for at in range(0, WIDTH, step):
        rows = slice(at, at + step)
        joint_grad[rows, :QKV] = dot_tn(normed[:, rows], grad_projected).astype(bf16)
        joint_grad[rows, QKV:PROJ_AT] = jnp.zeros((step, PROJ_AT - QKV), bf16)
        grad_rows = g_before[:, rows] + held[:, rows]
        joint_grad[rows, PROJ_AT:] = dot_tn(grad_rows, mixed[...]).astype(bf16)


def merge_kernel(_, blocks, weight, grad_act, merged, activated, grad_before, part):
    before = jnp.zeros((TOKENS, HIDDEN), f32)
    for quarter in range(QUARTERS):
        at = slice(quarter * WIDTH, (quarter + 1) * WIDTH)
        normed = unit_rows(blocks[quarter].astype(f32)).astype(bf16)
        merged[:, at] = normed
        before = before + dot(normed, weight[at, :])
    tail = 0.5 * (1.0 + lax.erf(before * math.sqrt(0.5)))
    bell = jnp.exp(-0.5 * before * before) * (1.0 / math.sqrt(2.0 * math.pi))
    activated[...] = (before * tail).astype(bf16)
    grad = ((tail + before * bell) * grad_act[...]).astype(bf16)
    grad_before[...] = grad
    for quarter in range(QUARTERS):
        at = slice(quarter * WIDTH, (quarter + 1) * WIDTH)
        part[quarter] = dot_nt(grad, weight[at, :]).astype(bf16)


def merger_grad_kernel(merged, grad_before, activated, visual_grad, out):
    out[0, :, :FEATURES] = dot_tn(activated[...], visual_grad[0]).astype(bf16)
    out[0, :, FEATURES:] = dot_tn(merged[0], grad_before[...]).astype(bf16)


def merger_grads(merged, grad_before, activated, visual_grad):
    whole = pl.BlockSpec((TOKENS, HIDDEN), lambda j: (0, 0))
    return pl.pallas_call(
        merger_grad_kernel,
        grid=(16,),
        in_specs=[
            pl.BlockSpec((1, TOKENS, HIDDEN), lambda j: (j, 0, 0)),
            whole,
            whole,
            pl.BlockSpec((1, TOKENS, FEATURES), lambda j: (j, 0, 0)),
        ],
        out_specs=pl.BlockSpec((1, HIDDEN, FEATURES + HIDDEN), lambda j: (j, 0, 0)),
        out_shape=jax.ShapeDtypeStruct((16, HIDDEN, FEATURES + HIDDEN), bf16),
        compiler_params=pltpu.CompilerParams(vmem_limit_bytes=16 * 1024 * 1024),
        cost_estimate=pl.CostEstimate(
            flops=2 * TOKENS * 16 * HIDDEN * (FEATURES + HIDDEN),
            bytes_accessed=4 * 16 * HIDDEN * (FEATURES + HIDDEN),
            transcendentals=0,
        ),
    )(merged, grad_before, activated, visual_grad)


def call(kernel, operands, results, scratch, flops, moved):
    return pl.pallas_call(
        kernel,
        in_specs=[pl.BlockSpec(memory_space=pltpu.SMEM)]
        + [pl.BlockSpec(memory_space=pltpu.VMEM)] * (len(operands) - 1),
        out_specs=[pl.BlockSpec(memory_space=pltpu.VMEM)] * len(results),
        out_shape=[jax.ShapeDtypeStruct(shape, kind) for shape, kind in results],
        scratch_shapes=[pltpu.VMEM(shape, kind) for shape, kind in scratch],
        compiler_params=pltpu.CompilerParams(vmem_limit_bytes=40 * 1024 * 1024),
        cost_estimate=pl.CostEstimate(flops=flops, bytes_accessed=moved, transcendentals=0),
    )(*operands)


PART = ((QUARTERS, TOKENS, WIDTH), bf16)


def local(
    patches,
    image_sizes,
    raster_order,
    image_starts,
    qkv_weight,
    proj_weight,
    merge_in,
    merge_out,
    text_embeds,
    joined_grad,
):
    section = lax.axis_index("section")
    place = lax.axis_index("mp")
    place_ref = place.reshape(1)
    is_last = section == SECTIONS - 1

    joint_local = jnp.concatenate(
        [qkv_weight[0], jnp.zeros((WIDTH // 16, PROJ_AT - QKV), bf16), proj_weight[0].T], axis=1
    )
    joint = lax.all_gather(joint_local, "dp", axis=0, tiled=True)

    marks = []
    spots = []
    for micro in range(2):
        image_of, within, onehot = image_layout(image_sizes[micro, 0])
        window_of = image_of * MERGED + within // WINDOW
        marks.append(jnp.where(is_last, image_of, window_of) + micro * 1024)
        starts = jnp.where(onehot, image_starts[micro, 0][None, :], 0)
        slots = jnp.sum(starts, axis=1, dtype=jnp.int32) + within
        order = raster_order[micro]
        from_raster = order[None, :] == jnp.arange(MERGED, dtype=jnp.int32)[:, None]
        spots.append(jnp.sum(jnp.where(from_raster, slots[None, :], 0), axis=1, dtype=jnp.int32))
    mark = jnp.tile(jnp.concatenate(marks), QUARTERS)
    down, right = mark[:, None], mark[None, :]
    positions = jnp.arange(text_embeds.shape[1], dtype=jnp.int32)
    chosen = jnp.stack(spots)[:, :, None] == positions[None, None, :]
    chosen_bf = chosen.astype(bf16)

    visual_grad = jnp.einsum(
        "mts,msf->mtf", chosen_bf, joined_grad, preferred_element_type=f32
    ).astype(bf16)
    visual_grad = visual_grad.reshape(TOKENS, FEATURES)
    visual_grad_full = lax.all_gather(visual_grad, ("section", "mp"), axis=0)
    grad_act = jnp.einsum(
        "jtf,rjf->tr",
        visual_grad_full,
        merge_out.reshape(HIDDEN, 16, FEATURES),
        preferred_element_type=f32,
    )

    quarters = jnp.swapaxes(patches.reshape(TOKENS, QUARTERS, WIDTH), 0, 1)
    quarters, visual_grad_full, grad_act = lax.optimization_barrier(
        (quarters, visual_grad_full, grad_act)
    )
    first = section == 0
    blocks = [quarters[quarter] for quarter in range(QUARTERS)]
    own = lax.dynamic_index_in_dim(quarters, place, 0, False)
    saved = [
        lax.dynamic_index_in_dim(quarters, (place + QUARTERS - step) % QUARTERS, 0, False)
        for step in range(QUARTERS)
    ]
    saved = [jnp.where(first, block, jnp.zeros_like(block)) for block in saved]

    layer_flops = 2 * ROWS * WIDTH * JOINT
    layer_bytes = 2 * WIDTH * JOINT + 8 * ROWS * WIDTH
    held = ((ROWS, WIDTH), bf16)
    for stage in range(SECTIONS):
        (terms,) = call(
            functools.partial(forward_kernel, turned=stage > 0),
            [place_ref, down, right, *blocks, joint],
            [PART],
            [held],
            layer_flops,
            layer_bytes,
        )
        total = own.astype(f32) + jnp.sum(exchange(terms).astype(f32), axis=0)
        own = total.astype(bf16)
        if stage < SECTIONS - 1:
            blocks = to_section(own, stage, stage + 1)
            saved = [old + new for old, new in zip(saved, blocks)]
            own = blocks[0]

    sent = [permute(own, across(SECTIONS - 1, target)) for target in range(SECTIONS - 1)]
    own = jnp.where(is_last, own, sent[0] + sent[1] + sent[2])
    merged, activated, grad_before, terms = call(
        merge_kernel,
        [place_ref, everyones(own), merge_in, grad_act],
        [
            ((TOKENS, QUARTERS * WIDTH), bf16),
            ((TOKENS, HIDDEN), bf16),
            ((TOKENS, HIDDEN), bf16),
            PART,
        ],
        [],
        4 * TOKENS * QUARTERS * WIDTH * HIDDEN,
        2 * QUARTERS * WIDTH * HIDDEN,
    )
    normed, projected, mixed = call(
        keep_kernel,
        [place_ref, down, right, *saved, joint],
        [((ROWS, WIDTH), bf16), ((ROWS, QKV), bf16), ((ROWS, MIX), bf16)],
        [held],
        layer_flops,
        layer_bytes,
    )

    total = jnp.sum(exchange(terms).astype(f32), axis=0)
    leaving = total.astype(bf16)
    leaving, merged, normed = lax.optimization_barrier((leaving, merged, normed))
    arrived = [permute(leaving, across(s, SECTIONS - 1)) for s in range(SECTIONS - 1)]
    merged = jnp.swapaxes(merged.reshape(TOKENS, 16, HIDDEN), 0, 1)
    merger_grad = merger_grads(merged, grad_before, activated, visual_grad_full)
    *arrived, merger_grad = lax.optimization_barrier((*arrived, merger_grad))
    merger_grad = lax.psum_scatter(merger_grad, "dp", scatter_dimension=0, tiled=False)
    for term in arrived:
        total = total + term.astype(f32)
    grad_own = unit_back(own.astype(f32), total)
    grad_own = jnp.where(is_last, grad_own, 0.0).astype(bf16)

    grad_rows = jnp.zeros((ROWS, WIDTH), bf16)
    grad_projected = jnp.zeros((ROWS, QKV), bf16)
    gathered = everyones(grad_own)
    grads = [gathered[quarter] for quarter in range(QUARTERS)]
    for layer in range(SECTIONS - 1, 0, -1):
        grad_rows, grad_projected, terms = call(
            functools.partial(backward_kernel, turned=layer < SECTIONS - 1),
            [place_ref, down, right, *grads, projected, joint, grad_rows, grad_projected],
            [((ROWS, WIDTH), bf16), ((ROWS, QKV), bf16), PART],
            [held],
            layer_flops,
            layer_bytes,
        )
        total = jnp.sum(exchange(terms).astype(f32), axis=0)
        grad_own = grad_own.astype(f32) + unit_back(saved[0].astype(f32), total)
        grads = to_section(grad_own.astype(bf16), layer, layer - 1)
        grad_own = grads[0]
    (joint_grad,) = call(
        last_kernel,
        [
            place_ref,
            down,
            right,
            *grads,
            projected,
            joint,
            grad_rows,
            grad_projected,
            normed,
            mixed,
        ],
        [((WIDTH, JOINT), bf16)],
        [held],
        2 * layer_flops,
        2 * layer_bytes,
    )
    reduced = lax.psum_scatter(joint_grad, "dp", scatter_dimension=0, tiled=True)
    qkv_grad = reduced[:, :QKV].astype(f32)
    proj_grad = reduced[:, PROJ_AT:].T.astype(f32)

    activated, joint_grad = lax.optimization_barrier((activated, joint_grad))
    visual_terms = jnp.einsum(
        "tr,rjf->jtf",
        activated,
        merge_out.reshape(HIDDEN, 16, FEATURES),
        preferred_element_type=f32,
    ).astype(bf16)
    visual = lax.all_to_all(visual_terms, ("section", "mp"), 0, 0)
    visual = jnp.sum(visual.astype(f32), axis=0).astype(bf16).reshape(2, MERGED, FEATURES)
    placed = jnp.einsum("mts,mtf->msf", chosen_bf, visual, preferred_element_type=f32)
    taken = jnp.any(chosen, axis=1)[:, :, None]
    joined = jnp.where(taken, placed.astype(bf16), text_embeds)
    merge_out_grad = merger_grad[:, :FEATURES].astype(f32)
    merge_in_grad = merger_grad[:, FEATURES:].astype(f32)
    return (joined, qkv_grad[None], proj_grad[None], merge_in_grad, merge_out_grad)


def solution(mesh):
    return jax.shard_map(
        local,
        mesh=mesh,
        in_specs=(
            P(None, "dp", None),
            P(None, "dp", None),
            P(None, "dp"),
            P(None, "dp", None),
            P("section", "dp", "mp"),
            P("section", "mp", "dp"),
            P(None, ("section", "mp")),
            P(("section", "mp"), None),
            P(None, "dp", ("section", "mp")),
            P(None, "dp", ("section", "mp")),
        ),
        out_specs=(
            P(None, "dp", ("section", "mp")),
            P("section", "dp", "mp"),
            P("section", "mp", "dp"),
            P("dp", ("section", "mp")),
            P(("section", "mp"), "dp"),
        ),
        check_vma=False,
    )
```

```python
import functools
import math

import jax
import jax.numpy as jnp
from jax import lax
from jax.experimental import pallas as pl
from jax.experimental.pallas import tpu as pltpu
from jax.sharding import PartitionSpec as P

HEADS_VIS = 16
WINDOW = 16
EPSILON = 1e-06

QUARTERS = 4
SECTIONS = 4
RANKS = 16
CHIPS = RANKS // 2
HEADS = HEADS_VIS // QUARTERS
HEAD = 80
WIDTH = 1280
MERGED = 24
TOKENS = 2 * MERGED
ROWS = QUARTERS * TOKENS
QKV = 3 * HEADS * HEAD
MIX = HEADS * HEAD
PROJ_AT = 1024
JOINT = PROJ_AT + MIX
HIDDEN = 320
FEATURES = 512
SHARE = WIDTH // RANKS
UPWARD = 640
SCALE = HEAD ** (-0.5)

bf16 = jnp.bfloat16
f32 = jnp.float32


def permute(value, pairs):
    return lax.ppermute(value, ("section", "mp"), pairs)


def across(source, target, steps=0):
    return [
        (QUARTERS * source + m, QUARTERS * target + (m + steps) % QUARTERS)
        for m in range(QUARTERS)
    ]


def to_section(value, source, target):
    return [permute(value, across(source, target, step)) for step in range(QUARTERS)]


def exchange(value):
    return lax.all_to_all(value, "mp", 0, 0)


def along_z(value, steps):
    return lax.ppermute(value, "dp", [(i, (i + 2 * steps) % RANKS) for i in range(RANKS)])


def pick(array, at):
    return lax.dynamic_index_in_dim(array, at, 0, False)


def everyones(value):
    return exchange(jnp.broadcast_to(value[None], (QUARTERS, *value.shape)))


def dot(a, b):
    return lax.dot_general(a, b, (((1,), (0,)), ((), ())), preferred_element_type=f32)


def dot_nt(a, b):
    return lax.dot_general(a, b, (((1,), (1,)), ((), ())), preferred_element_type=f32)


def dot_tn(a, b):
    return lax.dot_general(a, b, (((0,), (0,)), ((), ())), preferred_element_type=f32)


def following(value, earlier):
    first = earlier[0, 0].astype(f32)
    return jnp.where(first == first, value, jnp.zeros_like(value))


def unit_rows(values):
    return values * lax.rsqrt(jnp.mean(values * values, axis=-1, keepdims=True) + EPSILON)


def unit_back(values, cotangent):
    inverse = lax.rsqrt(jnp.mean(values * values, axis=-1, keepdims=True) + EPSILON)
    along = jnp.mean(cotangent * values, axis=-1, keepdims=True)
    return inverse * cotangent - values * (inverse * inverse * inverse * along)


def image_layout(image_sizes):
    span_ends = jnp.cumsum(image_sizes, dtype=jnp.int32)
    span_starts = span_ends - image_sizes
    places = jnp.arange(MERGED, dtype=jnp.int32)
    image_of = jnp.sum(
        (places[:, None] >= span_ends[None, :]).astype(jnp.int32), axis=1, dtype=jnp.int32
    )
    onehot = image_of[:, None] == jnp.arange(image_sizes.shape[0], dtype=jnp.int32)[None, :]
    offset = jnp.sum(jnp.where(onehot, span_starts[None, :], 0), axis=1, dtype=jnp.int32)
    return (image_of, places - offset, onehot)


def gather_blocks(place_ref, blocks, held, turned):
    for step in range(QUARTERS):
        if turned:
            owner = lax.rem(place_ref[0] - step + QUARTERS, QUARTERS)
            rows = pl.ds(pl.multiple_of(owner * TOKENS, 16), TOKENS)
        else:
            rows = slice(step * TOKENS, (step + 1) * TOKENS)
        held[rows, :] = blocks[step][...]


def head_parts(projected, head):
    at = 3 * HEAD * head
    return (
        projected[:, at : at + HEAD],
        projected[:, at + HEAD : at + 2 * HEAD],
        projected[:, at + 2 * HEAD : at + 3 * HEAD],
    )


def head_weights(queries, keys, same):
    scores = jnp.where(same, dot_nt(queries, keys) * SCALE, -1000000000.0)
    raised = jnp.exp(scores - jnp.max(scores, axis=-1, keepdims=True))
    return raised / jnp.sum(raised, axis=-1, keepdims=True)


def inner_rows(held, weight, same):
    normed = unit_rows(held[...].astype(f32)).astype(bf16)
    projected = dot(normed, weight[:, :QKV]).astype(bf16)
    mixed = []
    for head in range(HEADS):
        queries, keys, values = head_parts(projected, head)
        mixed.append(dot(head_weights(queries, keys, same).astype(bf16), values).astype(bf16))
    return normed, projected, jnp.concatenate(mixed, axis=1)


def forward_kernel(place_ref, down, across_ref, x0, x1, x2, x3, weight, part, held, *, turned):
    gather_blocks(place_ref, (x0, x1, x2, x3), held, turned)
    same = down[...] == across_ref[...]
    _, _, mixed = inner_rows(held, weight, same)
    total = dot_nt(mixed, weight[:, PROJ_AT:]).astype(bf16)
    for quarter in range(QUARTERS):
        part[quarter] = total[quarter * TOKENS : (quarter + 1) * TOKENS]


def keep_kernel(place_ref, down, across_ref, x0, x1, x2, x3, weight, normed, projected, mixed, held):
    gather_blocks(place_ref, (x0, x1, x2, x3), held, True)
    same = down[...] == across_ref[...]
    normed[...], projected[...], mixed[...] = inner_rows(held, weight, same)


def grad_heads(grad_out, projected, weight, same):
    grad_mixed = dot(grad_out, weight[:, PROJ_AT:]).astype(bf16)
    pieces = []
    for head in range(HEADS):
        queries, keys, values = head_parts(projected, head)
        weights = head_weights(queries, keys, same)
        grad_head = grad_mixed[:, HEAD * head : HEAD * (head + 1)]
        grad_values = dot_tn(weights.astype(bf16), grad_head)
        grad_weights = dot_nt(grad_head, values).astype(bf16).astype(f32)
        centre = jnp.sum(grad_weights * weights, axis=-1, keepdims=True)
        grad_scores = (weights * (grad_weights - centre) * SCALE).astype(bf16)
        pieces += [dot(grad_scores, keys), dot_tn(grad_scores, queries), grad_values]
    return jnp.concatenate([piece.astype(bf16) for piece in pieces], axis=1)


def backward_kernel(
    place_ref,
    down,
    across_ref,
    g0,
    g1,
    g2,
    g3,
    projected,
    weight,
    g_after,
    p_after,
    part,
    held,
    *,
    turned,
):
    gather_blocks(place_ref, (g0, g1, g2, g3), held, turned)
    same = down[...] == across_ref[...]
    grad_out = held[...]
    grad_projected = grad_heads(grad_out, projected[...], weight, same)
    total = dot_nt(grad_projected, weight[:, :QKV]).astype(bf16)
    for quarter in range(QUARTERS):
        part[quarter] = total[quarter * TOKENS : (quarter + 1) * TOKENS]
    g_after[...] = grad_out
    p_after[...] = grad_projected


def last_kernel(
    place_ref,
    down,
    across_ref,
    g0,
    g1,
    g2,
    g3,
    projected,
    weight,
    g_before,
    p_before,
    normed,
    mixed,
    keep_up,
    keep_down,
    give_up,
    give_down,
    held,
):
    gather_blocks(place_ref, (g0, g1, g2, g3), held, True)
    same = down[...] == across_ref[...]
    grad_projected = p_before[...] + grad_heads(held[...], projected[...], weight, same)
    held[...] = g_before[...] + held[...]
    even = place_ref[1] == 0
    spot = place_ref[2]
    half = WIDTH // 2
    gap = jnp.zeros((SHARE, PROJ_AT - QKV), bf16)
    for part in range(2):
        cols = slice(half * part, half * (part + 1))
        grad_qkv = dot_tn(normed[:, cols], grad_projected).astype(bf16)
        grad_proj = dot_tn(held[:, cols], mixed[...]).astype(bf16)
        for pair in range(CHIPS // 2):
            chip = CHIPS // 2 * part + pair
            up_slot = lax.rem(spot - 1 - chip + 2 * CHIPS, CHIPS)
            down_slot = lax.rem(chip - spot - 1 + 2 * CHIPS, CHIPS)
            top = slice(2 * SHARE * pair, 2 * SHARE * pair + SHARE)
            low = slice(2 * SHARE * pair + SHARE, 2 * SHARE * (pair + 1))
            kept_qkv = jnp.where(even, grad_qkv[top], grad_qkv[low])
            kept_proj = jnp.where(even, grad_proj[top], grad_proj[low])
            gone_qkv = jnp.where(even, grad_qkv[low], grad_qkv[top])
            gone_proj = jnp.where(even, grad_proj[low], grad_proj[top])
            for up, falling, qkv, proj in (
                (keep_up, keep_down, kept_qkv, kept_proj),
                (give_up, give_down, gone_qkv, gone_proj),
            ):
                up[up_slot] = qkv[:, :UPWARD]
                falling[down_slot, :, : QKV - UPWARD] = qkv[:, UPWARD:]
                falling[down_slot, :, QKV - UPWARD : PROJ_AT - UPWARD] = gap
                falling[down_slot, :, PROJ_AT - UPWARD :] = proj


def merge_kernel(_, blocks, weight, grad_act, merged, activated, grad_before, part):
    before = jnp.zeros((TOKENS, HIDDEN), f32)
    for quarter in range(QUARTERS):
        at = slice(quarter * WIDTH, (quarter + 1) * WIDTH)
        normed = unit_rows(blocks[quarter].astype(f32)).astype(bf16)
        for part_at in range(4):
            merged[4 * quarter + part_at] = normed[:, HIDDEN * part_at : HIDDEN * (part_at + 1)]
        before = before + dot_nt(normed, weight[:, at])
    tail = 0.5 * (1.0 + lax.erf(before * math.sqrt(0.5)))
    bell = jnp.exp(-0.5 * before * before) * (1.0 / math.sqrt(2.0 * math.pi))
    activated[...] = (before * tail).astype(bf16)
    grad = ((tail + before * bell) * grad_act[...]).astype(bf16)
    grad_before[...] = grad
    for quarter in range(QUARTERS):
        at = slice(quarter * WIDTH, (quarter + 1) * WIDTH)
        part[quarter] = dot(grad, weight[:, at]).astype(bf16)


def merger_grad_kernel(merged, grad_before, activated, visual_grad, out):
    out[0, :, :FEATURES] = dot_tn(activated[...], visual_grad[0]).astype(bf16)
    out[0, :, FEATURES:] = dot_tn(merged[0], grad_before[...]).astype(bf16)


def visual_kernel(activated, weight, out):
    out[0] = dot(activated[...], weight[...]).astype(bf16)


def visual_products(activated, merge_out):
    return pl.pallas_call(
        visual_kernel,
        grid=(16,),
        in_specs=[
            pl.BlockSpec((TOKENS, HIDDEN), lambda j: (0, 0)),
            pl.BlockSpec(
                (HIDDEN, FEATURES),
                lambda j: (0, lax.rem(j, SECTIONS) * QUARTERS + lax.div(j, SECTIONS)),
            ),
        ],
        out_specs=pl.BlockSpec((1, TOKENS, FEATURES), lambda j: (j, 0, 0)),
        out_shape=jax.ShapeDtypeStruct((16, TOKENS, FEATURES), bf16),
        compiler_params=pltpu.CompilerParams(vmem_limit_bytes=16 * 1024 * 1024),
        cost_estimate=pl.CostEstimate(
            flops=2 * TOKENS * HIDDEN * 16 * FEATURES,
            bytes_accessed=2 * HIDDEN * 16 * FEATURES,
            transcendentals=0,
        ),
    )(activated, merge_out)


def merger_grads(merged, grad_before, activated, visual_grad):
    whole = pl.BlockSpec((TOKENS, HIDDEN), lambda j: (0, 0))
    return pl.pallas_call(
        merger_grad_kernel,
        grid=(16,),
        in_specs=[
            pl.BlockSpec((1, TOKENS, HIDDEN), lambda j: (j, 0, 0)),
            whole,
            whole,
            pl.BlockSpec((1, TOKENS, FEATURES), lambda j: (j, 0, 0)),
        ],
        out_specs=pl.BlockSpec((1, HIDDEN, FEATURES + HIDDEN), lambda j: (j, 0, 0)),
        out_shape=jax.ShapeDtypeStruct((16, HIDDEN, FEATURES + HIDDEN), bf16),
        compiler_params=pltpu.CompilerParams(vmem_limit_bytes=16 * 1024 * 1024),
        cost_estimate=pl.CostEstimate(
            flops=2 * TOKENS * 16 * HIDDEN * (FEATURES + HIDDEN),
            bytes_accessed=4 * 16 * HIDDEN * (FEATURES + HIDDEN),
            transcendentals=0,
        ),
    )(merged, grad_before, activated, visual_grad)


def call(kernel, operands, results, scratch, flops, moved):
    return pl.pallas_call(
        kernel,
        in_specs=[pl.BlockSpec(memory_space=pltpu.SMEM)]
        + [pl.BlockSpec(memory_space=pltpu.VMEM)] * (len(operands) - 1),
        out_specs=[pl.BlockSpec(memory_space=pltpu.VMEM)] * len(results),
        out_shape=[jax.ShapeDtypeStruct(shape, kind) for shape, kind in results],
        scratch_shapes=[pltpu.VMEM(shape, kind) for shape, kind in scratch],
        compiler_params=pltpu.CompilerParams(vmem_limit_bytes=40 * 1024 * 1024),
        cost_estimate=pl.CostEstimate(flops=flops, bytes_accessed=moved, transcendentals=0),
    )(*operands)


PART = ((QUARTERS, TOKENS, WIDTH), bf16)


def local(
    patches,
    image_sizes,
    raster_order,
    image_starts,
    qkv_weight,
    proj_weight,
    merge_in,
    merge_out,
    text_embeds,
    joined_grad,
):
    section = lax.axis_index("section")
    place = lax.axis_index("mp")
    rank = lax.axis_index("dp")
    place_ref = jnp.stack([place, rank % 2, rank // 2])
    is_last = section == SECTIONS - 1

    joint_local = jnp.concatenate(
        [qkv_weight[0], jnp.zeros((WIDTH // 16, PROJ_AT - QKV), bf16), proj_weight[0].T], axis=1
    )
    joint = lax.all_gather(joint_local, "dp", axis=0, tiled=True)

    marks = []
    spots = []
    for micro in range(2):
        image_of, within, onehot = image_layout(image_sizes[micro, 0])
        window_of = image_of * MERGED + within // WINDOW
        marks.append(jnp.where(is_last, image_of, window_of) + micro * 1024)
        starts = jnp.where(onehot, image_starts[micro, 0][None, :], 0)
        slots = jnp.sum(starts, axis=1, dtype=jnp.int32) + within
        order = raster_order[micro]
        from_raster = order[None, :] == jnp.arange(MERGED, dtype=jnp.int32)[:, None]
        spots.append(jnp.sum(jnp.where(from_raster, slots[None, :], 0), axis=1, dtype=jnp.int32))
    mark = jnp.tile(jnp.concatenate(marks), QUARTERS)
    down, right = mark[:, None], mark[None, :]
    positions = jnp.arange(text_embeds.shape[1], dtype=jnp.int32)
    chosen = jnp.stack(spots)[:, :, None] == positions[None, None, :]
    chosen_bf = chosen.astype(bf16)

    visual_grad = jnp.einsum(
        "mts,msf->mtf", chosen_bf, joined_grad, preferred_element_type=f32
    ).astype(bf16)
    visual_grad = visual_grad.reshape(TOKENS, FEATURES)
    visual_grad_full = lax.all_gather(visual_grad, ("section", "mp"), axis=0)
    grad_act = jnp.einsum(
        "jtf,rjf->tr",
        visual_grad_full,
        merge_out.reshape(HIDDEN, 16, FEATURES),
        preferred_element_type=f32,
    )

    quarters = jnp.swapaxes(patches.reshape(TOKENS, QUARTERS, WIDTH), 0, 1)
    place_ref, visual_grad_full, grad_act = lax.optimization_barrier(
        (place_ref, visual_grad_full, grad_act)
    )
    first = section == 0
    blocks = [quarters[quarter] for quarter in range(QUARTERS)]
    own = lax.dynamic_index_in_dim(quarters, place, 0, False)
    saved = [
        lax.dynamic_index_in_dim(quarters, (place + QUARTERS - step) % QUARTERS, 0, False)
        for step in range(QUARTERS)
    ]
    saved = [jnp.where(first, block, jnp.zeros_like(block)) for block in saved]

    layer_flops = 2 * ROWS * WIDTH * JOINT
    layer_bytes = 2 * WIDTH * JOINT + 8 * ROWS * WIDTH
    held = ((ROWS, WIDTH), bf16)
    for stage in range(SECTIONS):
        (terms,) = call(
            functools.partial(forward_kernel, turned=stage > 0),
            [place_ref, down, right, *blocks, joint],
            [PART],
            [held],
            layer_flops,
            layer_bytes,
        )
        total = own.astype(f32) + jnp.sum(exchange(terms).astype(f32), axis=0)
        own = total.astype(bf16)
        if stage < SECTIONS - 1:
            blocks = to_section(own, stage, stage + 1)
            saved = [old + new for old, new in zip(saved, blocks)]
            own = blocks[0]

    sent = [permute(own, across(SECTIONS - 1, target)) for target in range(SECTIONS - 1)]
    own = jnp.where(is_last, own, sent[0] + sent[1] + sent[2])
    merged, activated, grad_before, terms = call(
        merge_kernel,
        [place_ref, everyones(own), merge_in.T, grad_act],
        [
            ((16, TOKENS, HIDDEN), bf16),
            ((TOKENS, HIDDEN), bf16),
            ((TOKENS, HIDDEN), bf16),
            PART,
        ],
        [],
        4 * TOKENS * QUARTERS * WIDTH * HIDDEN,
        2 * QUARTERS * WIDTH * HIDDEN,
    )
    normed, projected, mixed = call(
        keep_kernel,
        [place_ref, down, right, *saved, joint],
        [((ROWS, WIDTH), bf16), ((ROWS, QKV), bf16), ((ROWS, MIX), bf16)],
        [held],
        layer_flops,
        layer_bytes,
    )

    total = jnp.sum(exchange(terms).astype(f32), axis=0)
    leaving = total.astype(bf16)
    arrived = [permute(leaving, across(s, SECTIONS - 1)) for s in range(SECTIONS - 1)]
    for term in arrived:
        total = total + term.astype(f32)
    grad_own = unit_back(own.astype(f32), total)
    grad_own = jnp.where(is_last, grad_own, 0.0).astype(bf16)

    grad_rows = jnp.zeros((ROWS, WIDTH), bf16)
    grad_projected = jnp.zeros((ROWS, QKV), bf16)
    gathered = everyones(grad_own)
    grads = [gathered[quarter] for quarter in range(QUARTERS)]
    for layer in range(SECTIONS - 1, 0, -1):
        layer_rows, layer_projected, terms = call(
            functools.partial(backward_kernel, turned=layer < SECTIONS - 1),
            [place_ref, down, right, *grads, projected, joint],
            [((ROWS, WIDTH), bf16), ((ROWS, QKV), bf16), PART],
            [held],
            layer_flops,
            layer_bytes,
        )
        total = jnp.sum(exchange(terms).astype(f32), axis=0)
        grad_own = grad_own.astype(f32) + unit_back(saved[0].astype(f32), total)
        grad_own = grad_own.astype(bf16)
        after = grad_own
        if layer == 3:
            merged, after = lax.optimization_barrier((merged, after))
            beside = merger_grads(merged, grad_before, activated, visual_grad_full)
        elif layer == 2:
            activated, after = lax.optimization_barrier((activated, after))
            beside = visual_products(activated, merge_out)
        grads = to_section(after, layer, layer - 1)
        mine = section == layer
        grad_rows = jnp.where(mine, layer_rows, grad_rows)
        grad_projected = jnp.where(mine, layer_projected, grad_projected)
        if layer > 1:
            place_ref, beside = lax.optimization_barrier((place_ref, beside))
        grad_own = grads[0]
        if layer == 3:
            merger_grad = lax.psum_scatter(beside, "dp", scatter_dimension=0, tiled=False)
        elif layer == 2:
            visual = beside.reshape(QUARTERS, SECTIONS, TOKENS, FEATURES)
    keep_up, keep_down, give_up, give_down = call(
        last_kernel,
        [
            place_ref,
            down,
            right,
            *grads,
            projected,
            joint,
            grad_rows,
            grad_projected,
            normed,
            mixed,
        ],
        [((CHIPS, SHARE, UPWARD), bf16), ((CHIPS, SHARE, JOINT - UPWARD), bf16)] * 2,
        [held],
        2 * layer_flops,
        2 * layer_bytes,
    )
    other = [(i, i ^ 1) for i in range(RANKS)]
    given_up, given_down = lax.ppermute(give_up, "dp", other), lax.ppermute(give_down, "dp", other)
    given_up, merger_grad = lax.optimization_barrier((given_up, merger_grad))
    visual = following(visual, merger_grad)
    visual = lax.psum_scatter(visual, "mp", scatter_dimension=0, tiled=False)

    def add(total, keep, given, step):
        share = keep[step].astype(f32) + given[step].astype(f32)
        return share if total is None else total.astype(f32) + share

    up, falling = add(None, keep_up, given_up, 0), add(None, keep_down, given_down, 0)
    for step in range(1, CHIPS):
        up = add(along_z(up.astype(bf16), 1), keep_up, given_up, step)
        falling = add(along_z(falling.astype(bf16), -1), keep_down, given_down, step)
        if step == 4:
            visual = following(visual, up)
            terms = [pick(visual, (section + turn) % SECTIONS) for turn in range(SECTIONS)]
            visual = terms[0].astype(f32)
            for turn in range(1, SECTIONS):
                pairs = [(s, (s + turn) % SECTIONS) for s in range(SECTIONS)]
                visual = visual + lax.ppermute(terms[turn], "section", pairs).astype(f32)
            visual = visual.astype(bf16)
    reduced = jnp.concatenate([up, falling], axis=1)
    qkv_grad = reduced[:, :QKV]
    proj_grad = reduced[:, PROJ_AT:].T
    visual = visual.reshape(2, MERGED, FEATURES)
    placed = jnp.einsum("mts,mtf->msf", chosen_bf, visual, preferred_element_type=f32)
    taken = jnp.any(chosen, axis=1)[:, :, None]
    joined = jnp.where(taken, placed.astype(bf16), text_embeds)
    merge_out_grad = merger_grad[:, :FEATURES].astype(f32)
    merge_in_grad = merger_grad[:, FEATURES:].astype(f32)
    return (joined, qkv_grad[None], proj_grad[None], merge_in_grad, merge_out_grad)


def solution(mesh):
    return jax.shard_map(
        local,
        mesh=mesh,
        in_specs=(
            P(None, "dp", None),
            P(None, "dp", None),
            P(None, "dp"),
            P(None, "dp", None),
            P("section", "dp", "mp"),
            P("section", "mp", "dp"),
            P(None, ("section", "mp")),
            P(("section", "mp"), None),
            P(None, "dp", ("section", "mp")),
            P(None, "dp", ("section", "mp")),
        ),
        out_specs=(
            P(None, "dp", ("section", "mp")),
            P("section", "dp", "mp"),
            P("section", "mp", "dp"),
            P("dp", ("section", "mp")),
            P(("section", "mp"), "dp"),
        ),
        check_vma=False,
    )
```

```python
import functools
import math

import jax
import jax.numpy as jnp
from jax import lax
from jax.experimental import pallas as pl
from jax.experimental.pallas import tpu as pltpu
from jax.sharding import PartitionSpec as P

HEADS_VIS = 16
WINDOW = 16
EPSILON = 1e-06

QUARTERS = 4
SECTIONS = 4
HEADS = HEADS_VIS // QUARTERS
HEAD = 80
WIDTH = 1280
MERGED = 24
TOKENS = 2 * MERGED
ROWS = QUARTERS * TOKENS
QKV = 3 * HEADS * HEAD
MIX = HEADS * HEAD
PROJ_AT = 1024
JOINT = PROJ_AT + MIX
HIDDEN = 320
FEATURES = 512
SCALE = HEAD ** (-0.5)

bf16 = jnp.bfloat16
f32 = jnp.float32


def permute(value, pairs):
    return lax.ppermute(value, ("section", "mp"), pairs)


def across(source, target, steps=0):
    return [
        (QUARTERS * source + m, QUARTERS * target + (m + steps) % QUARTERS)
        for m in range(QUARTERS)
    ]


def to_section(value, source, target):
    return [permute(value, across(source, target, step)) for step in range(QUARTERS)]


def exchange(value):
    return lax.all_to_all(value, "mp", 0, 0)


def everyones(value):
    return exchange(jnp.broadcast_to(value[None], (QUARTERS, *value.shape)))


def dot(a, b):
    return lax.dot_general(a, b, (((1,), (0,)), ((), ())), preferred_element_type=f32)


def dot_nt(a, b):
    return lax.dot_general(a, b, (((1,), (1,)), ((), ())), preferred_element_type=f32)


def dot_tn(a, b):
    return lax.dot_general(a, b, (((0,), (0,)), ((), ())), preferred_element_type=f32)


def unit_rows(values):
    return values * lax.rsqrt(jnp.mean(values * values, axis=-1, keepdims=True) + EPSILON)


def unit_back(values, cotangent):
    inverse = lax.rsqrt(jnp.mean(values * values, axis=-1, keepdims=True) + EPSILON)
    along = jnp.mean(cotangent * values, axis=-1, keepdims=True)
    return inverse * cotangent - values * (inverse * inverse * inverse * along)


def image_layout(image_sizes):
    span_ends = jnp.cumsum(image_sizes, dtype=jnp.int32)
    span_starts = span_ends - image_sizes
    places = jnp.arange(MERGED, dtype=jnp.int32)
    image_of = jnp.sum(
        (places[:, None] >= span_ends[None, :]).astype(jnp.int32), axis=1, dtype=jnp.int32
    )
    onehot = image_of[:, None] == jnp.arange(image_sizes.shape[0], dtype=jnp.int32)[None, :]
    offset = jnp.sum(jnp.where(onehot, span_starts[None, :], 0), axis=1, dtype=jnp.int32)
    return (image_of, places - offset, onehot)


def gather_blocks(place_ref, blocks, held, turned):
    for step in range(QUARTERS):
        if turned:
            owner = lax.rem(place_ref[0] - step + QUARTERS, QUARTERS)
            rows = pl.ds(pl.multiple_of(owner * TOKENS, 16), TOKENS)
        else:
            rows = slice(step * TOKENS, (step + 1) * TOKENS)
        held[rows, :] = blocks[step][...]


def head_parts(projected, head):
    at = 3 * HEAD * head
    return (
        projected[:, at : at + HEAD],
        projected[:, at + HEAD : at + 2 * HEAD],
        projected[:, at + 2 * HEAD : at + 3 * HEAD],
    )


def head_weights(queries, keys, same):
    scores = jnp.where(same, dot_nt(queries, keys) * SCALE, -1000000000.0)
    raised = jnp.exp(scores - jnp.max(scores, axis=-1, keepdims=True))
    return raised / jnp.sum(raised, axis=-1, keepdims=True)


def inner_rows(held, weight, same):
    normed = unit_rows(held[...].astype(f32)).astype(bf16)
    projected = dot(normed, weight[:, :QKV]).astype(bf16)
    mixed = []
    for head in range(HEADS):
        queries, keys, values = head_parts(projected, head)
        mixed.append(dot(head_weights(queries, keys, same).astype(bf16), values).astype(bf16))
    return normed, projected, jnp.concatenate(mixed, axis=1)


def forward_kernel(place_ref, down, across_ref, x0, x1, x2, x3, weight, part, held, *, turned):
    gather_blocks(place_ref, (x0, x1, x2, x3), held, turned)
    same = down[...] == across_ref[...]
    _, _, mixed = inner_rows(held, weight, same)
    total = dot_nt(mixed, weight[:, PROJ_AT:]).astype(bf16)
    for quarter in range(QUARTERS):
        part[quarter] = total[quarter * TOKENS : (quarter + 1) * TOKENS]


def keep_kernel(place_ref, down, across_ref, x0, x1, x2, x3, weight, normed, projected, mixed, held):
    gather_blocks(place_ref, (x0, x1, x2, x3), held, True)
    same = down[...] == across_ref[...]
    normed[...], projected[...], mixed[...] = inner_rows(held, weight, same)


def grad_heads(grad_out, projected, weight, same):
    grad_mixed = dot(grad_out, weight[:, PROJ_AT:]).astype(bf16)
    pieces = []
    for head in range(HEADS):
        queries, keys, values = head_parts(projected, head)
        weights = head_weights(queries, keys, same)
        grad_head = grad_mixed[:, HEAD * head : HEAD * (head + 1)]
        grad_values = dot_tn(weights.astype(bf16), grad_head)
        grad_weights = dot_nt(grad_head, values).astype(bf16).astype(f32)
        centre = jnp.sum(grad_weights * weights, axis=-1, keepdims=True)
        grad_scores = (weights * (grad_weights - centre) * SCALE).astype(bf16)
        pieces += [dot(grad_scores, keys), dot_tn(grad_scores, queries), grad_values]
    return jnp.concatenate([piece.astype(bf16) for piece in pieces], axis=1)


def backward_kernel(
    place_ref,
    down,
    across_ref,
    g0,
    g1,
    g2,
    g3,
    projected,
    weight,
    g_before,
    p_before,
    g_after,
    p_after,
    part,
    held,
    *,
    turned,
):
    gather_blocks(place_ref, (g0, g1, g2, g3), held, turned)
    same = down[...] == across_ref[...]
    grad_out = held[...]
    grad_projected = grad_heads(grad_out, projected[...], weight, same)
    total = dot_nt(grad_projected, weight[:, :QKV]).astype(bf16)
    for quarter in range(QUARTERS):
        part[quarter] = total[quarter * TOKENS : (quarter + 1) * TOKENS]
    g_after[...] = g_before[...] + grad_out
    p_after[...] = p_before[...] + grad_projected


def last_kernel(
    place_ref,
    down,
    across_ref,
    g0,
    g1,
    g2,
    g3,
    projected,
    weight,
    g_before,
    p_before,
    normed,
    mixed,
    joint_grad,
    held,
):
    gather_blocks(place_ref, (g0, g1, g2, g3), held, True)
    same = down[...] == across_ref[...]
    grad_projected = p_before[...] + grad_heads(held[...], projected[...], weight, same)
    step = WIDTH // 5
    for at in range(0, WIDTH, step):
        rows = slice(at, at + step)
        joint_grad[rows, :QKV] = dot_tn(normed[:, rows], grad_projected).astype(bf16)
        joint_grad[rows, QKV:PROJ_AT] = jnp.zeros((step, PROJ_AT - QKV), bf16)
        grad_rows = g_before[:, rows] + held[:, rows]
        joint_grad[rows, PROJ_AT:] = dot_tn(grad_rows, mixed[...]).astype(bf16)


def merge_kernel(_, blocks, weight, grad_act, merged, activated, grad_before, part):
    before = jnp.zeros((TOKENS, HIDDEN), f32)
    for quarter in range(QUARTERS):
        at = slice(quarter * WIDTH, (quarter + 1) * WIDTH)
        normed = unit_rows(blocks[quarter].astype(f32)).astype(bf16)
        for part_at in range(4):
            merged[4 * quarter + part_at] = normed[:, HIDDEN * part_at : HIDDEN * (part_at + 1)]
        before = before + dot_nt(normed, weight[:, at])
    tail = 0.5 * (1.0 + lax.erf(before * math.sqrt(0.5)))
    bell = jnp.exp(-0.5 * before * before) * (1.0 / math.sqrt(2.0 * math.pi))
    activated[...] = (before * tail).astype(bf16)
    grad = ((tail + before * bell) * grad_act[...]).astype(bf16)
    grad_before[...] = grad
    for quarter in range(QUARTERS):
        at = slice(quarter * WIDTH, (quarter + 1) * WIDTH)
        part[quarter] = dot(grad, weight[:, at]).astype(bf16)


def merger_grad_kernel(merged, grad_before, activated, visual_grad, out):
    out[0, :, :FEATURES] = dot_tn(activated[...], visual_grad[0]).astype(bf16)
    out[0, :, FEATURES:] = dot_tn(merged[0], grad_before[...]).astype(bf16)


def merger_grads(merged, grad_before, activated, visual_grad):
    whole = pl.BlockSpec((TOKENS, HIDDEN), lambda j: (0, 0))
    return pl.pallas_call(
        merger_grad_kernel,
        grid=(16,),
        in_specs=[
            pl.BlockSpec((1, TOKENS, HIDDEN), lambda j: (j, 0, 0)),
            whole,
            whole,
            pl.BlockSpec((1, TOKENS, FEATURES), lambda j: (j, 0, 0)),
        ],
        out_specs=pl.BlockSpec((1, HIDDEN, FEATURES + HIDDEN), lambda j: (j, 0, 0)),
        out_shape=jax.ShapeDtypeStruct((16, HIDDEN, FEATURES + HIDDEN), bf16),
        compiler_params=pltpu.CompilerParams(vmem_limit_bytes=16 * 1024 * 1024),
        cost_estimate=pl.CostEstimate(
            flops=2 * TOKENS * 16 * HIDDEN * (FEATURES + HIDDEN),
            bytes_accessed=4 * 16 * HIDDEN * (FEATURES + HIDDEN),
            transcendentals=0,
        ),
    )(merged, grad_before, activated, visual_grad)


def call(kernel, operands, results, scratch, flops, moved):
    return pl.pallas_call(
        kernel,
        in_specs=[pl.BlockSpec(memory_space=pltpu.SMEM)]
        + [pl.BlockSpec(memory_space=pltpu.VMEM)] * (len(operands) - 1),
        out_specs=[pl.BlockSpec(memory_space=pltpu.VMEM)] * len(results),
        out_shape=[jax.ShapeDtypeStruct(shape, kind) for shape, kind in results],
        scratch_shapes=[pltpu.VMEM(shape, kind) for shape, kind in scratch],
        compiler_params=pltpu.CompilerParams(vmem_limit_bytes=40 * 1024 * 1024),
        cost_estimate=pl.CostEstimate(flops=flops, bytes_accessed=moved, transcendentals=0),
    )(*operands)


PART = ((QUARTERS, TOKENS, WIDTH), bf16)


def local(
    patches,
    image_sizes,
    raster_order,
    image_starts,
    qkv_weight,
    proj_weight,
    merge_in,
    merge_out,
    text_embeds,
    joined_grad,
):
    section = lax.axis_index("section")
    place = lax.axis_index("mp")
    place_ref = place.reshape(1)
    is_last = section == SECTIONS - 1

    joint_local = jnp.concatenate(
        [qkv_weight[0], jnp.zeros((WIDTH // 16, PROJ_AT - QKV), bf16), proj_weight[0].T], axis=1
    )
    joint = lax.all_gather(joint_local, "dp", axis=0, tiled=True)

    marks = []
    spots = []
    for micro in range(2):
        image_of, within, onehot = image_layout(image_sizes[micro, 0])
        window_of = image_of * MERGED + within // WINDOW
        marks.append(jnp.where(is_last, image_of, window_of) + micro * 1024)
        starts = jnp.where(onehot, image_starts[micro, 0][None, :], 0)
        slots = jnp.sum(starts, axis=1, dtype=jnp.int32) + within
        order = raster_order[micro]
        from_raster = order[None, :] == jnp.arange(MERGED, dtype=jnp.int32)[:, None]
        spots.append(jnp.sum(jnp.where(from_raster, slots[None, :], 0), axis=1, dtype=jnp.int32))
    mark = jnp.tile(jnp.concatenate(marks), QUARTERS)
    down, right = mark[:, None], mark[None, :]
    positions = jnp.arange(text_embeds.shape[1], dtype=jnp.int32)
    chosen = jnp.stack(spots)[:, :, None] == positions[None, None, :]
    chosen_bf = chosen.astype(bf16)

    visual_grad = jnp.einsum(
        "mts,msf->mtf", chosen_bf, joined_grad, preferred_element_type=f32
    ).astype(bf16)
    visual_grad = visual_grad.reshape(TOKENS, FEATURES)
    visual_grad_full = lax.all_gather(visual_grad, ("section", "mp"), axis=0)
    grad_act = jnp.einsum(
        "jtf,rjf->tr",
        visual_grad_full,
        merge_out.reshape(HIDDEN, 16, FEATURES),
        preferred_element_type=f32,
    )

    quarters = jnp.swapaxes(patches.reshape(TOKENS, QUARTERS, WIDTH), 0, 1)
    quarters, visual_grad_full, grad_act = lax.optimization_barrier(
        (quarters, visual_grad_full, grad_act)
    )
    first = section == 0
    blocks = [quarters[quarter] for quarter in range(QUARTERS)]
    own = lax.dynamic_index_in_dim(quarters, place, 0, False)
    saved = [
        lax.dynamic_index_in_dim(quarters, (place + QUARTERS - step) % QUARTERS, 0, False)
        for step in range(QUARTERS)
    ]
    saved = [jnp.where(first, block, jnp.zeros_like(block)) for block in saved]

    layer_flops = 2 * ROWS * WIDTH * JOINT
    layer_bytes = 2 * WIDTH * JOINT + 8 * ROWS * WIDTH
    held = ((ROWS, WIDTH), bf16)
    for stage in range(SECTIONS):
        (terms,) = call(
            functools.partial(forward_kernel, turned=stage > 0),
            [place_ref, down, right, *blocks, joint],
            [PART],
            [held],
            layer_flops,
            layer_bytes,
        )
        total = own.astype(f32) + jnp.sum(exchange(terms).astype(f32), axis=0)
        own = total.astype(bf16)
        if stage < SECTIONS - 1:
            blocks = to_section(own, stage, stage + 1)
            saved = [old + new for old, new in zip(saved, blocks)]
            own = blocks[0]

    sent = [permute(own, across(SECTIONS - 1, target)) for target in range(SECTIONS - 1)]
    own = jnp.where(is_last, own, sent[0] + sent[1] + sent[2])
    merged, activated, grad_before, terms = call(
        merge_kernel,
        [place_ref, everyones(own), merge_in.T, grad_act],
        [
            ((16, TOKENS, HIDDEN), bf16),
            ((TOKENS, HIDDEN), bf16),
            ((TOKENS, HIDDEN), bf16),
            PART,
        ],
        [],
        4 * TOKENS * QUARTERS * WIDTH * HIDDEN,
        2 * QUARTERS * WIDTH * HIDDEN,
    )
    normed, projected, mixed = call(
        keep_kernel,
        [place_ref, down, right, *saved, joint],
        [((ROWS, WIDTH), bf16), ((ROWS, QKV), bf16), ((ROWS, MIX), bf16)],
        [held],
        layer_flops,
        layer_bytes,
    )

    total = jnp.sum(exchange(terms).astype(f32), axis=0)
    leaving = total.astype(bf16)
    arrived = [permute(leaving, across(s, SECTIONS - 1)) for s in range(SECTIONS - 1)]
    for term in arrived:
        total = total + term.astype(f32)
    grad_own = unit_back(own.astype(f32), total)
    grad_own = jnp.where(is_last, grad_own, 0.0).astype(bf16)

    grad_rows = jnp.zeros((ROWS, WIDTH), bf16)
    grad_projected = jnp.zeros((ROWS, QKV), bf16)
    gathered = everyones(grad_own)
    grads = [gathered[quarter] for quarter in range(QUARTERS)]
    for layer in range(SECTIONS - 1, 0, -1):
        grad_rows, grad_projected, terms = call(
            functools.partial(backward_kernel, turned=layer < SECTIONS - 1),
            [place_ref, down, right, *grads, projected, joint, grad_rows, grad_projected],
            [((ROWS, WIDTH), bf16), ((ROWS, QKV), bf16), PART],
            [held],
            layer_flops,
            layer_bytes,
        )
        total = jnp.sum(exchange(terms).astype(f32), axis=0)
        grad_own = grad_own.astype(f32) + unit_back(saved[0].astype(f32), total)
        grad_own = grad_own.astype(bf16)
        if layer == SECTIONS - 1:
            merged, grad_own = lax.optimization_barrier((merged, grad_own))
            merger_grad = merger_grads(merged, grad_before, activated, visual_grad_full)
        grads = to_section(grad_own, layer, layer - 1)
        if layer == SECTIONS - 1:
            place_ref, merger_grad = lax.optimization_barrier((place_ref, merger_grad))
            merger_grad = lax.psum_scatter(
                merger_grad, "dp", scatter_dimension=0, tiled=False
            )
        grad_own = grads[0]
    (joint_grad,) = call(
        last_kernel,
        [
            place_ref,
            down,
            right,
            *grads,
            projected,
            joint,
            grad_rows,
            grad_projected,
            normed,
            mixed,
        ],
        [((WIDTH, JOINT), bf16)],
        [held],
        2 * layer_flops,
        2 * layer_bytes,
    )
    joint_grad, merger_grad = lax.optimization_barrier((joint_grad, merger_grad))
    reduced = lax.psum_scatter(joint_grad, "dp", scatter_dimension=0, tiled=True)
    qkv_grad = reduced[:, :QKV].astype(f32)
    proj_grad = reduced[:, PROJ_AT:].T.astype(f32)

    activated, joint_grad = lax.optimization_barrier((activated, joint_grad))
    visual_terms = jnp.einsum(
        "tr,rjf->jtf",
        activated,
        merge_out.reshape(HIDDEN, 16, FEATURES),
        preferred_element_type=f32,
    ).astype(bf16)
    visual = lax.all_to_all(visual_terms, ("section", "mp"), 0, 0)
    visual = jnp.sum(visual.astype(f32), axis=0).astype(bf16).reshape(2, MERGED, FEATURES)
    placed = jnp.einsum("mts,mtf->msf", chosen_bf, visual, preferred_element_type=f32)
    taken = jnp.any(chosen, axis=1)[:, :, None]
    joined = jnp.where(taken, placed.astype(bf16), text_embeds)
    merge_out_grad = merger_grad[:, :FEATURES].astype(f32)
    merge_in_grad = merger_grad[:, FEATURES:].astype(f32)
    return (joined, qkv_grad[None], proj_grad[None], merge_in_grad, merge_out_grad)


def solution(mesh):
    return jax.shard_map(
        local,
        mesh=mesh,
        in_specs=(
            P(None, "dp", None),
            P(None, "dp", None),
            P(None, "dp"),
            P(None, "dp", None),
            P("section", "dp", "mp"),
            P("section", "mp", "dp"),
            P(None, ("section", "mp")),
            P(("section", "mp"), None),
            P(None, "dp", ("section", "mp")),
            P(None, "dp", ("section", "mp")),
        ),
        out_specs=(
            P(None, "dp", ("section", "mp")),
            P("section", "dp", "mp"),
            P("section", "mp", "dp"),
            P("dp", ("section", "mp")),
            P(("section", "mp"), "dp"),
        ),
        check_vma=False,
    )
```

```python
import functools
import math

import jax
import jax.numpy as jnp
from jax import lax
from jax.experimental import pallas as pl
from jax.experimental.pallas import tpu as pltpu
from jax.sharding import PartitionSpec as P

HEADS_VIS = 16
WINDOW = 16
EPSILON = 1e-06

QUARTERS = 4
SECTIONS = 4
HEADS = HEADS_VIS // QUARTERS
HEAD = 80
WIDTH = 1280
MERGED = 24
TOKENS = 2 * MERGED
ROWS = QUARTERS * TOKENS
QKV = 3 * HEADS * HEAD
MIX = HEADS * HEAD
PROJ_AT = 1024
JOINT = PROJ_AT + MIX
HIDDEN = 320
FEATURES = 512
SCALE = HEAD ** (-0.5)

bf16 = jnp.bfloat16
f32 = jnp.float32


def permute(value, pairs):
    return lax.ppermute(value, ("section", "mp"), pairs)


def across(source, target, steps=0):
    return [
        (QUARTERS * source + m, QUARTERS * target + (m + steps) % QUARTERS)
        for m in range(QUARTERS)
    ]


def to_section(value, source, target):
    return [permute(value, across(source, target, step)) for step in range(QUARTERS)]


def exchange(value):
    return lax.all_to_all(value, "mp", 0, 0)


def everyones(value):
    return exchange(jnp.broadcast_to(value[None], (QUARTERS, *value.shape)))


def dot(a, b):
    return lax.dot_general(a, b, (((1,), (0,)), ((), ())), preferred_element_type=f32)


def dot_nt(a, b):
    return lax.dot_general(a, b, (((1,), (1,)), ((), ())), preferred_element_type=f32)


def dot_tn(a, b):
    return lax.dot_general(a, b, (((0,), (0,)), ((), ())), preferred_element_type=f32)


def unit_rows(values):
    return values * lax.rsqrt(jnp.mean(values * values, axis=-1, keepdims=True) + EPSILON)


def unit_back(values, cotangent):
    inverse = lax.rsqrt(jnp.mean(values * values, axis=-1, keepdims=True) + EPSILON)
    along = jnp.mean(cotangent * values, axis=-1, keepdims=True)
    return inverse * cotangent - values * (inverse * inverse * inverse * along)


def image_layout(image_sizes):
    span_ends = jnp.cumsum(image_sizes, dtype=jnp.int32)
    span_starts = span_ends - image_sizes
    places = jnp.arange(MERGED, dtype=jnp.int32)
    image_of = jnp.sum(
        (places[:, None] >= span_ends[None, :]).astype(jnp.int32), axis=1, dtype=jnp.int32
    )
    onehot = image_of[:, None] == jnp.arange(image_sizes.shape[0], dtype=jnp.int32)[None, :]
    offset = jnp.sum(jnp.where(onehot, span_starts[None, :], 0), axis=1, dtype=jnp.int32)
    return (image_of, places - offset, onehot)


def gather_blocks(place_ref, blocks, held, turned):
    for step in range(QUARTERS):
        if turned:
            owner = lax.rem(place_ref[0] - step + QUARTERS, QUARTERS)
            rows = pl.ds(pl.multiple_of(owner * TOKENS, 16), TOKENS)
        else:
            rows = slice(step * TOKENS, (step + 1) * TOKENS)
        held[rows, :] = blocks[step][...]


def head_parts(projected, head):
    at = 3 * HEAD * head
    return (
        projected[:, at : at + HEAD],
        projected[:, at + HEAD : at + 2 * HEAD],
        projected[:, at + 2 * HEAD : at + 3 * HEAD],
    )


def head_weights(queries, keys, same):
    scores = jnp.where(same, dot_nt(queries, keys) * SCALE, -1000000000.0)
    raised = jnp.exp(scores - jnp.max(scores, axis=-1, keepdims=True))
    return raised / jnp.sum(raised, axis=-1, keepdims=True)


def inner_rows(held, weight, same):
    normed = unit_rows(held[...].astype(f32)).astype(bf16)
    projected = dot(normed, weight[:, :QKV]).astype(bf16)
    mixed = []
    for head in range(HEADS):
        queries, keys, values = head_parts(projected, head)
        mixed.append(dot(head_weights(queries, keys, same).astype(bf16), values).astype(bf16))
    return normed, projected, jnp.concatenate(mixed, axis=1)


def forward_kernel(place_ref, down, across_ref, x0, x1, x2, x3, weight, part, held, *, turned):
    gather_blocks(place_ref, (x0, x1, x2, x3), held, turned)
    same = down[...] == across_ref[...]
    _, _, mixed = inner_rows(held, weight, same)
    total = dot_nt(mixed, weight[:, PROJ_AT:]).astype(bf16)
    for quarter in range(QUARTERS):
        part[quarter] = total[quarter * TOKENS : (quarter + 1) * TOKENS]


def keep_kernel(place_ref, down, across_ref, x0, x1, x2, x3, weight, normed, projected, mixed, held):
    gather_blocks(place_ref, (x0, x1, x2, x3), held, True)
    same = down[...] == across_ref[...]
    normed[...], projected[...], mixed[...] = inner_rows(held, weight, same)


def grad_heads(grad_out, projected, weight, same):
    grad_mixed = dot(grad_out, weight[:, PROJ_AT:]).astype(bf16)
    pieces = []
    for head in range(HEADS):
        queries, keys, values = head_parts(projected, head)
        weights = head_weights(queries, keys, same)
        grad_head = grad_mixed[:, HEAD * head : HEAD * (head + 1)]
        grad_values = dot_tn(weights.astype(bf16), grad_head)
        grad_weights = dot_nt(grad_head, values).astype(bf16).astype(f32)
        centre = jnp.sum(grad_weights * weights, axis=-1, keepdims=True)
        grad_scores = (weights * (grad_weights - centre) * SCALE).astype(bf16)
        pieces += [dot(grad_scores, keys), dot_tn(grad_scores, queries), grad_values]
    return jnp.concatenate([piece.astype(bf16) for piece in pieces], axis=1)


def backward_kernel(
    place_ref,
    down,
    across_ref,
    g0,
    g1,
    g2,
    g3,
    projected,
    weight,
    g_before,
    p_before,
    g_after,
    p_after,
    part,
    held,
    *,
    turned,
):
    gather_blocks(place_ref, (g0, g1, g2, g3), held, turned)
    same = down[...] == across_ref[...]
    grad_out = held[...]
    grad_projected = grad_heads(grad_out, projected[...], weight, same)
    total = dot_nt(grad_projected, weight[:, :QKV]).astype(bf16)
    for quarter in range(QUARTERS):
        part[quarter] = total[quarter * TOKENS : (quarter + 1) * TOKENS]
    g_after[...] = g_before[...] + grad_out
    p_after[...] = p_before[...] + grad_projected


def last_kernel(
    place_ref,
    down,
    across_ref,
    g0,
    g1,
    g2,
    g3,
    projected,
    weight,
    g_before,
    p_before,
    normed,
    mixed,
    joint_grad,
    held,
):
    gather_blocks(place_ref, (g0, g1, g2, g3), held, True)
    same = down[...] == across_ref[...]
    grad_projected = p_before[...] + grad_heads(held[...], projected[...], weight, same)
    step = WIDTH // 5
    for at in range(0, WIDTH, step):
        rows = slice(at, at + step)
        joint_grad[rows, :QKV] = dot_tn(normed[:, rows], grad_projected).astype(bf16)
        joint_grad[rows, QKV:PROJ_AT] = jnp.zeros((step, PROJ_AT - QKV), bf16)
        grad_rows = g_before[:, rows] + held[:, rows]
        joint_grad[rows, PROJ_AT:] = dot_tn(grad_rows, mixed[...]).astype(bf16)


def merge_kernel(_, blocks, weight, grad_act, merged, activated, grad_before, part):
    before = jnp.zeros((TOKENS, HIDDEN), f32)
    for quarter in range(QUARTERS):
        at = slice(quarter * WIDTH, (quarter + 1) * WIDTH)
        normed = unit_rows(blocks[quarter].astype(f32)).astype(bf16)
        for part_at in range(4):
            merged[4 * quarter + part_at] = normed[:, HIDDEN * part_at : HIDDEN * (part_at + 1)]
        before = before + dot_nt(normed, weight[:, at])
    tail = 0.5 * (1.0 + lax.erf(before * math.sqrt(0.5)))
    bell = jnp.exp(-0.5 * before * before) * (1.0 / math.sqrt(2.0 * math.pi))
    activated[...] = (before * tail).astype(bf16)
    grad = ((tail + before * bell) * grad_act[...]).astype(bf16)
    grad_before[...] = grad
    for quarter in range(QUARTERS):
        at = slice(quarter * WIDTH, (quarter + 1) * WIDTH)
        part[quarter] = dot(grad, weight[:, at]).astype(bf16)


def merger_grad_kernel(merged, grad_before, activated, visual_grad, out):
    out[0, :, :FEATURES] = dot_tn(activated[...], visual_grad[0]).astype(bf16)
    out[0, :, FEATURES:] = dot_tn(merged[0], grad_before[...]).astype(bf16)


def merger_grads(merged, grad_before, activated, visual_grad):
    whole = pl.BlockSpec((TOKENS, HIDDEN), lambda j: (0, 0))
    return pl.pallas_call(
        merger_grad_kernel,
        grid=(16,),
        in_specs=[
            pl.BlockSpec((1, TOKENS, HIDDEN), lambda j: (j, 0, 0)),
            whole,
            whole,
            pl.BlockSpec((1, TOKENS, FEATURES), lambda j: (j, 0, 0)),
        ],
        out_specs=pl.BlockSpec((1, HIDDEN, FEATURES + HIDDEN), lambda j: (j, 0, 0)),
        out_shape=jax.ShapeDtypeStruct((16, HIDDEN, FEATURES + HIDDEN), bf16),
        compiler_params=pltpu.CompilerParams(vmem_limit_bytes=16 * 1024 * 1024),
        cost_estimate=pl.CostEstimate(
            flops=2 * TOKENS * 16 * HIDDEN * (FEATURES + HIDDEN),
            bytes_accessed=4 * 16 * HIDDEN * (FEATURES + HIDDEN),
            transcendentals=0,
        ),
    )(merged, grad_before, activated, visual_grad)


def call(kernel, operands, results, scratch, flops, moved):
    return pl.pallas_call(
        kernel,
        in_specs=[pl.BlockSpec(memory_space=pltpu.SMEM)]
        + [pl.BlockSpec(memory_space=pltpu.VMEM)] * (len(operands) - 1),
        out_specs=[pl.BlockSpec(memory_space=pltpu.VMEM)] * len(results),
        out_shape=[jax.ShapeDtypeStruct(shape, kind) for shape, kind in results],
        scratch_shapes=[pltpu.VMEM(shape, kind) for shape, kind in scratch],
        compiler_params=pltpu.CompilerParams(vmem_limit_bytes=40 * 1024 * 1024),
        cost_estimate=pl.CostEstimate(flops=flops, bytes_accessed=moved, transcendentals=0),
    )(*operands)


PART = ((QUARTERS, TOKENS, WIDTH), bf16)


def local(
    patches,
    image_sizes,
    raster_order,
    image_starts,
    qkv_weight,
    proj_weight,
    merge_in,
    merge_out,
    text_embeds,
    joined_grad,
):
    section = lax.axis_index("section")
    place = lax.axis_index("mp")
    place_ref = place.reshape(1)
    is_last = section == SECTIONS - 1

    joint_local = jnp.concatenate(
        [qkv_weight[0], jnp.zeros((WIDTH // 16, PROJ_AT - QKV), bf16), proj_weight[0].T], axis=1
    )
    joint = lax.all_gather(joint_local, "dp", axis=0, tiled=True)

    marks = []
    spots = []
    for micro in range(2):
        image_of, within, onehot = image_layout(image_sizes[micro, 0])
        window_of = image_of * MERGED + within // WINDOW
        marks.append(jnp.where(is_last, image_of, window_of) + micro * 1024)
        starts = jnp.where(onehot, image_starts[micro, 0][None, :], 0)
        slots = jnp.sum(starts, axis=1, dtype=jnp.int32) + within
        order = raster_order[micro]
        from_raster = order[None, :] == jnp.arange(MERGED, dtype=jnp.int32)[:, None]
        spots.append(jnp.sum(jnp.where(from_raster, slots[None, :], 0), axis=1, dtype=jnp.int32))
    mark = jnp.tile(jnp.concatenate(marks), QUARTERS)
    down, right = mark[:, None], mark[None, :]
    positions = jnp.arange(text_embeds.shape[1], dtype=jnp.int32)
    chosen = jnp.stack(spots)[:, :, None] == positions[None, None, :]
    chosen_bf = chosen.astype(bf16)

    visual_grad = jnp.einsum(
        "mts,msf->mtf", chosen_bf, joined_grad, preferred_element_type=f32
    ).astype(bf16)
    visual_grad = visual_grad.reshape(TOKENS, FEATURES)
    visual_grad_full = lax.all_gather(visual_grad, ("section", "mp"), axis=0)
    grad_act = jnp.einsum(
        "jtf,rjf->tr",
        visual_grad_full,
        merge_out.reshape(HIDDEN, 16, FEATURES),
        preferred_element_type=f32,
    )

    quarters = jnp.swapaxes(patches.reshape(TOKENS, QUARTERS, WIDTH), 0, 1)
    quarters, visual_grad_full, grad_act = lax.optimization_barrier(
        (quarters, visual_grad_full, grad_act)
    )
    first = section == 0
    blocks = [quarters[quarter] for quarter in range(QUARTERS)]
    own = lax.dynamic_index_in_dim(quarters, place, 0, False)
    saved = [
        lax.dynamic_index_in_dim(quarters, (place + QUARTERS - step) % QUARTERS, 0, False)
        for step in range(QUARTERS)
    ]
    saved = [jnp.where(first, block, jnp.zeros_like(block)) for block in saved]

    layer_flops = 2 * ROWS * WIDTH * JOINT
    layer_bytes = 2 * WIDTH * JOINT + 8 * ROWS * WIDTH
    held = ((ROWS, WIDTH), bf16)
    for stage in range(SECTIONS):
        (terms,) = call(
            functools.partial(forward_kernel, turned=stage > 0),
            [place_ref, down, right, *blocks, joint],
            [PART],
            [held],
            layer_flops,
            layer_bytes,
        )
        total = own.astype(f32) + jnp.sum(exchange(terms).astype(f32), axis=0)
        own = total.astype(bf16)
        if stage < SECTIONS - 1:
            blocks = to_section(own, stage, stage + 1)
            saved = [old + new for old, new in zip(saved, blocks)]
            own = blocks[0]

    sent = [permute(own, across(SECTIONS - 1, target)) for target in range(SECTIONS - 1)]
    own = jnp.where(is_last, own, sent[0] + sent[1] + sent[2])
    merged, activated, grad_before, terms = call(
        merge_kernel,
        [place_ref, everyones(own), merge_in.T, grad_act],
        [
            ((16, TOKENS, HIDDEN), bf16),
            ((TOKENS, HIDDEN), bf16),
            ((TOKENS, HIDDEN), bf16),
            PART,
        ],
        [],
        4 * TOKENS * QUARTERS * WIDTH * HIDDEN,
        2 * QUARTERS * WIDTH * HIDDEN,
    )
    normed, projected, mixed = call(
        keep_kernel,
        [place_ref, down, right, *saved, joint],
        [((ROWS, WIDTH), bf16), ((ROWS, QKV), bf16), ((ROWS, MIX), bf16)],
        [held],
        layer_flops,
        layer_bytes,
    )

    total = jnp.sum(exchange(terms).astype(f32), axis=0)
    leaving = total.astype(bf16)
    leaving, merged, normed = lax.optimization_barrier((leaving, merged, normed))
    arrived = [permute(leaving, across(s, SECTIONS - 1)) for s in range(SECTIONS - 1)]
    merger_grad = merger_grads(merged, grad_before, activated, visual_grad_full)
    *arrived, merger_grad = lax.optimization_barrier((*arrived, merger_grad))
    merger_grad = lax.psum_scatter(merger_grad, "dp", scatter_dimension=0, tiled=False)
    for term in arrived:
        total = total + term.astype(f32)
    grad_own = unit_back(own.astype(f32), total)
    grad_own = jnp.where(is_last, grad_own, 0.0).astype(bf16)

    grad_rows = jnp.zeros((ROWS, WIDTH), bf16)
    grad_projected = jnp.zeros((ROWS, QKV), bf16)
    gathered = everyones(grad_own)
    grads = [gathered[quarter] for quarter in range(QUARTERS)]
    for layer in range(SECTIONS - 1, 0, -1):
        grad_rows, grad_projected, terms = call(
            functools.partial(backward_kernel, turned=layer < SECTIONS - 1),
            [place_ref, down, right, *grads, projected, joint, grad_rows, grad_projected],
            [((ROWS, WIDTH), bf16), ((ROWS, QKV), bf16), PART],
            [held],
            layer_flops,
            layer_bytes,
        )
        total = jnp.sum(exchange(terms).astype(f32), axis=0)
        grad_own = grad_own.astype(f32) + unit_back(saved[0].astype(f32), total)
        grad_own = grad_own.astype(bf16)
        grads = to_section(grad_own, layer, layer - 1)
        grad_own = grads[0]
    (joint_grad,) = call(
        last_kernel,
        [
            place_ref,
            down,
            right,
            *grads,
            projected,
            joint,
            grad_rows,
            grad_projected,
            normed,
            mixed,
        ],
        [((WIDTH, JOINT), bf16)],
        [held],
        2 * layer_flops,
        2 * layer_bytes,
    )
    joint_grad, merger_grad = lax.optimization_barrier((joint_grad, merger_grad))
    reduced = lax.psum_scatter(joint_grad, "dp", scatter_dimension=0, tiled=True)
    qkv_grad = reduced[:, :QKV].astype(f32)
    proj_grad = reduced[:, PROJ_AT:].T.astype(f32)

    activated, joint_grad = lax.optimization_barrier((activated, joint_grad))
    visual_terms = jnp.einsum(
        "tr,rjf->jtf",
        activated,
        merge_out.reshape(HIDDEN, 16, FEATURES),
        preferred_element_type=f32,
    ).astype(bf16)
    visual = lax.all_to_all(visual_terms, ("section", "mp"), 0, 0)
    visual = jnp.sum(visual.astype(f32), axis=0).astype(bf16).reshape(2, MERGED, FEATURES)
    placed = jnp.einsum("mts,mtf->msf", chosen_bf, visual, preferred_element_type=f32)
    taken = jnp.any(chosen, axis=1)[:, :, None]
    joined = jnp.where(taken, placed.astype(bf16), text_embeds)
    merge_out_grad = merger_grad[:, :FEATURES].astype(f32)
    merge_in_grad = merger_grad[:, FEATURES:].astype(f32)
    return (joined, qkv_grad[None], proj_grad[None], merge_in_grad, merge_out_grad)


def solution(mesh):
    return jax.shard_map(
        local,
        mesh=mesh,
        in_specs=(
            P(None, "dp", None),
            P(None, "dp", None),
            P(None, "dp"),
            P(None, "dp", None),
            P("section", "dp", "mp"),
            P("section", "mp", "dp"),
            P(None, ("section", "mp")),
            P(("section", "mp"), None),
            P(None, "dp", ("section", "mp")),
            P(None, "dp", ("section", "mp")),
        ),
        out_specs=(
            P(None, "dp", ("section", "mp")),
            P("section", "dp", "mp"),
            P("section", "mp", "dp"),
            P("dp", ("section", "mp")),
            P(("section", "mp"), "dp"),
        ),
        check_vma=False,
    )
```

```python
import functools
import math

import jax
import jax.numpy as jnp
from jax import lax
from jax.experimental import pallas as pl
from jax.experimental.pallas import tpu as pltpu
from jax.sharding import PartitionSpec as P

HEADS_VIS = 16
WINDOW = 16
EPSILON = 1e-06

QUARTERS = 4
SECTIONS = 4
HEADS = HEADS_VIS // QUARTERS
HEAD = 80
WIDTH = 1280
MERGED = 24
TOKENS = 2 * MERGED
ROWS = QUARTERS * TOKENS
QKV = 3 * HEADS * HEAD
MIX = HEADS * HEAD
PROJ_AT = 1024
JOINT = PROJ_AT + MIX
HIDDEN = 320
FEATURES = 512
SCALE = HEAD ** (-0.5)

bf16 = jnp.bfloat16
f32 = jnp.float32


def permute(value, pairs):
    return lax.ppermute(value, ("section", "mp"), pairs)


def across(source, target, steps=0):
    return [
        (QUARTERS * source + m, QUARTERS * target + (m + steps) % QUARTERS)
        for m in range(QUARTERS)
    ]


def to_section(value, source, target):
    return [permute(value, across(source, target, step)) for step in range(QUARTERS)]


def exchange(value):
    return lax.all_to_all(value, "mp", 0, 0)


def everyones(value):
    return exchange(jnp.broadcast_to(value[None], (QUARTERS, *value.shape)))


def dot(a, b):
    return lax.dot_general(a, b, (((1,), (0,)), ((), ())), preferred_element_type=f32)


def dot_nt(a, b):
    return lax.dot_general(a, b, (((1,), (1,)), ((), ())), preferred_element_type=f32)


def dot_tn(a, b):
    return lax.dot_general(a, b, (((0,), (0,)), ((), ())), preferred_element_type=f32)


def unit_rows(values):
    return values * lax.rsqrt(jnp.mean(values * values, axis=-1, keepdims=True) + EPSILON)


def unit_back(values, cotangent):
    inverse = lax.rsqrt(jnp.mean(values * values, axis=-1, keepdims=True) + EPSILON)
    along = jnp.mean(cotangent * values, axis=-1, keepdims=True)
    return inverse * cotangent - values * (inverse * inverse * inverse * along)


def image_layout(image_sizes):
    span_ends = jnp.cumsum(image_sizes, dtype=jnp.int32)
    span_starts = span_ends - image_sizes
    places = jnp.arange(MERGED, dtype=jnp.int32)
    image_of = jnp.sum(
        (places[:, None] >= span_ends[None, :]).astype(jnp.int32), axis=1, dtype=jnp.int32
    )
    onehot = image_of[:, None] == jnp.arange(image_sizes.shape[0], dtype=jnp.int32)[None, :]
    offset = jnp.sum(jnp.where(onehot, span_starts[None, :], 0), axis=1, dtype=jnp.int32)
    return (image_of, places - offset, onehot)


def gather_blocks(place_ref, blocks, held, turned):
    for step in range(QUARTERS):
        if turned:
            owner = lax.rem(place_ref[0] - step + QUARTERS, QUARTERS)
            rows = pl.ds(pl.multiple_of(owner * TOKENS, 16), TOKENS)
        else:
            rows = slice(step * TOKENS, (step + 1) * TOKENS)
        held[rows, :] = blocks[step][...]


def head_parts(projected, head):
    at = 3 * HEAD * head
    return (
        projected[:, at : at + HEAD],
        projected[:, at + HEAD : at + 2 * HEAD],
        projected[:, at + 2 * HEAD : at + 3 * HEAD],
    )


def head_weights(queries, keys, same):
    scores = jnp.where(same, dot_nt(queries, keys) * SCALE, -1000000000.0)
    raised = jnp.exp(scores - jnp.max(scores, axis=-1, keepdims=True))
    return raised / jnp.sum(raised, axis=-1, keepdims=True)


def inner_rows(held, weight, same):
    normed = unit_rows(held[...].astype(f32)).astype(bf16)
    projected = dot(normed, weight[:, :QKV]).astype(bf16)
    mixed = []
    for head in range(HEADS):
        queries, keys, values = head_parts(projected, head)
        mixed.append(dot(head_weights(queries, keys, same).astype(bf16), values).astype(bf16))
    return normed, projected, jnp.concatenate(mixed, axis=1)


def forward_kernel(place_ref, down, across_ref, x0, x1, x2, x3, weight, part, held, *, turned):
    gather_blocks(place_ref, (x0, x1, x2, x3), held, turned)
    same = down[...] == across_ref[...]
    _, _, mixed = inner_rows(held, weight, same)
    total = dot_nt(mixed, weight[:, PROJ_AT:]).astype(bf16)
    for quarter in range(QUARTERS):
        part[quarter] = total[quarter * TOKENS : (quarter + 1) * TOKENS]


def keep_kernel(place_ref, down, across_ref, x0, x1, x2, x3, weight, normed, projected, mixed, held):
    gather_blocks(place_ref, (x0, x1, x2, x3), held, True)
    same = down[...] == across_ref[...]
    normed[...], projected[...], mixed[...] = inner_rows(held, weight, same)


def grad_heads(grad_out, projected, weight, same):
    grad_mixed = dot(grad_out, weight[:, PROJ_AT:]).astype(bf16)
    pieces = []
    for head in range(HEADS):
        queries, keys, values = head_parts(projected, head)
        weights = head_weights(queries, keys, same)
        grad_head = grad_mixed[:, HEAD * head : HEAD * (head + 1)]
        grad_values = dot_tn(weights.astype(bf16), grad_head)
        grad_weights = dot_nt(grad_head, values).astype(bf16).astype(f32)
        centre = jnp.sum(grad_weights * weights, axis=-1, keepdims=True)
        grad_scores = (weights * (grad_weights - centre) * SCALE).astype(bf16)
        pieces += [dot(grad_scores, keys), dot_tn(grad_scores, queries), grad_values]
    return jnp.concatenate([piece.astype(bf16) for piece in pieces], axis=1)


def backward_kernel(
    place_ref,
    down,
    across_ref,
    g0,
    g1,
    g2,
    g3,
    projected,
    weight,
    g_before,
    p_before,
    g_after,
    p_after,
    part,
    held,
    *,
    turned,
):
    gather_blocks(place_ref, (g0, g1, g2, g3), held, turned)
    same = down[...] == across_ref[...]
    grad_out = held[...]
    grad_projected = grad_heads(grad_out, projected[...], weight, same)
    total = dot_nt(grad_projected, weight[:, :QKV]).astype(bf16)
    for quarter in range(QUARTERS):
        part[quarter] = total[quarter * TOKENS : (quarter + 1) * TOKENS]
    g_after[...] = g_before[...] + grad_out
    p_after[...] = p_before[...] + grad_projected


def last_kernel(
    place_ref,
    down,
    across_ref,
    g0,
    g1,
    g2,
    g3,
    projected,
    weight,
    g_before,
    p_before,
    normed,
    mixed,
    joint_grad,
    held,
):
    gather_blocks(place_ref, (g0, g1, g2, g3), held, True)
    same = down[...] == across_ref[...]
    grad_projected = p_before[...] + grad_heads(held[...], projected[...], weight, same)
    step = WIDTH // 5
    for at in range(0, WIDTH, step):
        rows = slice(at, at + step)
        joint_grad[rows, :QKV] = dot_tn(normed[:, rows], grad_projected).astype(bf16)
        joint_grad[rows, QKV:PROJ_AT] = jnp.zeros((step, PROJ_AT - QKV), bf16)
        grad_rows = g_before[:, rows] + held[:, rows]
        joint_grad[rows, PROJ_AT:] = dot_tn(grad_rows, mixed[...]).astype(bf16)


def merge_kernel(_, blocks, weight, grad_act, merged, activated, grad_before, part):
    before = jnp.zeros((TOKENS, HIDDEN), f32)
    for quarter in range(QUARTERS):
        at = slice(quarter * WIDTH, (quarter + 1) * WIDTH)
        normed = unit_rows(blocks[quarter].astype(f32)).astype(bf16)
        for part_at in range(4):
            merged[4 * quarter + part_at] = normed[:, HIDDEN * part_at : HIDDEN * (part_at + 1)]
        before = before + dot_nt(normed, weight[:, at])
    tail = 0.5 * (1.0 + lax.erf(before * math.sqrt(0.5)))
    bell = jnp.exp(-0.5 * before * before) * (1.0 / math.sqrt(2.0 * math.pi))
    activated[...] = (before * tail).astype(bf16)
    grad = ((tail + before * bell) * grad_act[...]).astype(bf16)
    grad_before[...] = grad
    for quarter in range(QUARTERS):
        at = slice(quarter * WIDTH, (quarter + 1) * WIDTH)
        part[quarter] = dot(grad, weight[:, at]).astype(bf16)


def merger_grad_kernel(merged, grad_before, activated, visual_grad, out):
    out[0, :, :FEATURES] = dot_tn(activated[...], visual_grad[0]).astype(bf16)
    out[0, :, FEATURES:] = dot_tn(merged[0], grad_before[...]).astype(bf16)


def merger_grads(merged, grad_before, activated, visual_grad):
    whole = pl.BlockSpec((TOKENS, HIDDEN), lambda j: (0, 0))
    return pl.pallas_call(
        merger_grad_kernel,
        grid=(16,),
        in_specs=[
            pl.BlockSpec((1, TOKENS, HIDDEN), lambda j: (j, 0, 0)),
            whole,
            whole,
            pl.BlockSpec((1, TOKENS, FEATURES), lambda j: (j, 0, 0)),
        ],
        out_specs=pl.BlockSpec((1, HIDDEN, FEATURES + HIDDEN), lambda j: (j, 0, 0)),
        out_shape=jax.ShapeDtypeStruct((16, HIDDEN, FEATURES + HIDDEN), bf16),
        compiler_params=pltpu.CompilerParams(vmem_limit_bytes=16 * 1024 * 1024),
        cost_estimate=pl.CostEstimate(
            flops=2 * TOKENS * 16 * HIDDEN * (FEATURES + HIDDEN),
            bytes_accessed=4 * 16 * HIDDEN * (FEATURES + HIDDEN),
            transcendentals=0,
        ),
    )(merged, grad_before, activated, visual_grad)


def call(kernel, operands, results, scratch, flops, moved):
    return pl.pallas_call(
        kernel,
        in_specs=[pl.BlockSpec(memory_space=pltpu.SMEM)]
        + [pl.BlockSpec(memory_space=pltpu.VMEM)] * (len(operands) - 1),
        out_specs=[pl.BlockSpec(memory_space=pltpu.VMEM)] * len(results),
        out_shape=[jax.ShapeDtypeStruct(shape, kind) for shape, kind in results],
        scratch_shapes=[pltpu.VMEM(shape, kind) for shape, kind in scratch],
        compiler_params=pltpu.CompilerParams(vmem_limit_bytes=48 * 1024 * 1024),
        cost_estimate=pl.CostEstimate(flops=flops, bytes_accessed=moved, transcendentals=0),
    )(*operands)


PART = ((QUARTERS, TOKENS, WIDTH), bf16)


def local(
    patches,
    image_sizes,
    raster_order,
    image_starts,
    qkv_weight,
    proj_weight,
    merge_in,
    merge_out,
    text_embeds,
    joined_grad,
):
    section = lax.axis_index("section")
    place = lax.axis_index("mp")
    place_ref = place.reshape(1)
    is_last = section == SECTIONS - 1

    joint_local = jnp.concatenate(
        [qkv_weight[0], jnp.zeros((WIDTH // 16, PROJ_AT - QKV), bf16), proj_weight[0].T], axis=1
    )
    joint = lax.all_gather(joint_local, "dp", axis=0, tiled=True)

    marks = []
    spots = []
    for micro in range(2):
        image_of, within, onehot = image_layout(image_sizes[micro, 0])
        window_of = image_of * MERGED + within // WINDOW
        marks.append(jnp.where(is_last, image_of, window_of) + micro * 1024)
        starts = jnp.where(onehot, image_starts[micro, 0][None, :], 0)
        slots = jnp.sum(starts, axis=1, dtype=jnp.int32) + within
        order = raster_order[micro]
        from_raster = order[None, :] == jnp.arange(MERGED, dtype=jnp.int32)[:, None]
        spots.append(jnp.sum(jnp.where(from_raster, slots[None, :], 0), axis=1, dtype=jnp.int32))
    mark = jnp.tile(jnp.concatenate(marks), QUARTERS)
    down, right = mark[:, None], mark[None, :]
    positions = jnp.arange(text_embeds.shape[1], dtype=jnp.int32)
    chosen = jnp.stack(spots)[:, :, None] == positions[None, None, :]
    chosen_bf = chosen.astype(bf16)

    visual_grad = jnp.einsum(
        "mts,msf->mtf", chosen_bf, joined_grad, preferred_element_type=f32
    ).astype(bf16)
    visual_grad = visual_grad.reshape(TOKENS, FEATURES)
    visual_grad_full = lax.all_gather(visual_grad, ("section", "mp"), axis=0)
    grad_act = jnp.einsum(
        "jtf,rjf->tr",
        visual_grad_full,
        merge_out.reshape(HIDDEN, 16, FEATURES),
        preferred_element_type=f32,
    )

    quarters = jnp.swapaxes(patches.reshape(TOKENS, QUARTERS, WIDTH), 0, 1)
    quarters, visual_grad_full, grad_act = lax.optimization_barrier(
        (quarters, visual_grad_full, grad_act)
    )
    first = section == 0
    blocks = [quarters[quarter] for quarter in range(QUARTERS)]
    own = lax.dynamic_index_in_dim(quarters, place, 0, False)
    saved = [
        lax.dynamic_index_in_dim(quarters, (place + QUARTERS - step) % QUARTERS, 0, False)
        for step in range(QUARTERS)
    ]
    saved = [jnp.where(first, block, jnp.zeros_like(block)) for block in saved]

    layer_flops = 2 * ROWS * WIDTH * JOINT
    layer_bytes = 2 * WIDTH * JOINT + 8 * ROWS * WIDTH
    held = ((ROWS, WIDTH), bf16)
    for stage in range(SECTIONS):
        (terms,) = call(
            functools.partial(forward_kernel, turned=stage > 0),
            [place_ref, down, right, *blocks, joint],
            [PART],
            [held],
            layer_flops,
            layer_bytes,
        )
        total = own.astype(f32) + jnp.sum(exchange(terms).astype(f32), axis=0)
        own = total.astype(bf16)
        if stage < SECTIONS - 1:
            blocks = to_section(own, stage, stage + 1)
            saved = [old + new for old, new in zip(saved, blocks)]
            own = blocks[0]

    sent = [permute(own, across(SECTIONS - 1, target)) for target in range(SECTIONS - 1)]
    own = jnp.where(is_last, own, sent[0] + sent[1] + sent[2])
    merged, activated, grad_before, terms = call(
        merge_kernel,
        [place_ref, everyones(own), merge_in.T, grad_act],
        [
            ((16, TOKENS, HIDDEN), bf16),
            ((TOKENS, HIDDEN), bf16),
            ((TOKENS, HIDDEN), bf16),
            PART,
        ],
        [],
        4 * TOKENS * QUARTERS * WIDTH * HIDDEN,
        2 * QUARTERS * WIDTH * HIDDEN,
    )
    normed, projected, mixed = call(
        keep_kernel,
        [place_ref, down, right, *saved, joint],
        [((ROWS, WIDTH), bf16), ((ROWS, QKV), bf16), ((ROWS, MIX), bf16)],
        [held],
        layer_flops,
        layer_bytes,
    )

    total = jnp.sum(exchange(terms).astype(f32), axis=0)
    leaving = total.astype(bf16)
    leaving, merged, normed = lax.optimization_barrier((leaving, merged, normed))
    arrived = [permute(leaving, across(s, SECTIONS - 1)) for s in range(SECTIONS - 1)]
    merger_grad = merger_grads(merged, grad_before, activated, visual_grad_full)
    *arrived, merger_grad = lax.optimization_barrier((*arrived, merger_grad))
    merger_grad = lax.psum_scatter(merger_grad, "dp", scatter_dimension=0, tiled=False)
    for term in arrived:
        total = total + term.astype(f32)
    grad_own = unit_back(own.astype(f32), total)
    grad_own = jnp.where(is_last, grad_own, 0.0).astype(bf16)

    grad_rows = jnp.zeros((ROWS, WIDTH), bf16)
    grad_projected = jnp.zeros((ROWS, QKV), bf16)
    gathered = everyones(grad_own)
    grads = [gathered[quarter] for quarter in range(QUARTERS)]
    for layer in range(SECTIONS - 1, 0, -1):
        grad_rows, grad_projected, terms = call(
            functools.partial(backward_kernel, turned=layer < SECTIONS - 1),
            [place_ref, down, right, *grads, projected, joint, grad_rows, grad_projected],
            [((ROWS, WIDTH), bf16), ((ROWS, QKV), bf16), PART],
            [held],
            layer_flops,
            layer_bytes,
        )
        total = jnp.sum(exchange(terms).astype(f32), axis=0)
        grad_own = grad_own.astype(f32) + unit_back(saved[0].astype(f32), total)
        grad_own = grad_own.astype(bf16)
        grads = to_section(grad_own, layer, layer - 1)
        grad_own = grads[0]
    (joint_grad,) = call(
        last_kernel,
        [
            place_ref,
            down,
            right,
            *grads,
            projected,
            joint,
            grad_rows,
            grad_projected,
            normed,
            mixed,
        ],
        [((WIDTH, JOINT), bf16)],
        [held],
        2 * layer_flops,
        2 * layer_bytes,
    )
    joint_grad, merger_grad = lax.optimization_barrier((joint_grad, merger_grad))
    reduced = lax.psum_scatter(joint_grad, "dp", scatter_dimension=0, tiled=True)
    qkv_grad = reduced[:, :QKV].astype(f32)
    proj_grad = reduced[:, PROJ_AT:].T.astype(f32)

    activated, joint_grad = lax.optimization_barrier((activated, joint_grad))
    visual_terms = jnp.einsum(
        "tr,rjf->jtf",
        activated,
        merge_out.reshape(HIDDEN, 16, FEATURES),
        preferred_element_type=f32,
    ).astype(bf16)
    visual = lax.all_to_all(visual_terms, ("section", "mp"), 0, 0)
    visual = jnp.sum(visual.astype(f32), axis=0).astype(bf16).reshape(2, MERGED, FEATURES)
    placed = jnp.einsum("mts,mtf->msf", chosen_bf, visual, preferred_element_type=f32)
    taken = jnp.any(chosen, axis=1)[:, :, None]
    joined = jnp.where(taken, placed.astype(bf16), text_embeds)
    merge_out_grad = merger_grad[:, :FEATURES].astype(f32)
    merge_in_grad = merger_grad[:, FEATURES:].astype(f32)
    return (joined, qkv_grad[None], proj_grad[None], merge_in_grad, merge_out_grad)


def solution(mesh):
    return jax.shard_map(
        local,
        mesh=mesh,
        in_specs=(
            P(None, "dp", None),
            P(None, "dp", None),
            P(None, "dp"),
            P(None, "dp", None),
            P("section", "dp", "mp"),
            P("section", "mp", "dp"),
            P(None, ("section", "mp")),
            P(("section", "mp"), None),
            P(None, "dp", ("section", "mp")),
            P(None, "dp", ("section", "mp")),
        ),
        out_specs=(
            P(None, "dp", ("section", "mp")),
            P("section", "dp", "mp"),
            P("section", "mp", "dp"),
            P("dp", ("section", "mp")),
            P(("section", "mp"), "dp"),
        ),
        check_vma=False,
    )
```

```python
import functools
import math

import jax
import jax.numpy as jnp
from jax import lax
from jax.experimental import pallas as pl
from jax.experimental.pallas import tpu as pltpu
from jax.sharding import PartitionSpec as P

HEADS_VIS = 16
WINDOW = 16
EPSILON = 1e-06

QUARTERS = 4
SECTIONS = 4
HEADS = HEADS_VIS // QUARTERS
HEAD = 80
WIDTH = 1280
MERGED = 24
TOKENS = 2 * MERGED
ROWS = QUARTERS * TOKENS
QKV = 3 * HEADS * HEAD
MIX = HEADS * HEAD
PROJ_AT = 1024
JOINT = PROJ_AT + MIX
HIDDEN = 320
FEATURES = 512
SCALE = HEAD ** (-0.5)

bf16 = jnp.bfloat16
f32 = jnp.float32


def permute(value, pairs):
    return lax.ppermute(value, ("section", "mp"), pairs)


def across(source, target, steps=0):
    return [
        (QUARTERS * source + m, QUARTERS * target + (m + steps) % QUARTERS)
        for m in range(QUARTERS)
    ]


def to_section(value, source, target):
    return [permute(value, across(source, target, step)) for step in range(QUARTERS)]


def exchange(value):
    return lax.all_to_all(value, "mp", 0, 0)


def everyones(value):
    return exchange(jnp.broadcast_to(value[None], (QUARTERS, *value.shape)))


def dot(a, b):
    return lax.dot_general(a, b, (((1,), (0,)), ((), ())), preferred_element_type=f32)


def dot_nt(a, b):
    return lax.dot_general(a, b, (((1,), (1,)), ((), ())), preferred_element_type=f32)


def dot_tn(a, b):
    return lax.dot_general(a, b, (((0,), (0,)), ((), ())), preferred_element_type=f32)


def unit_rows(values):
    return values * lax.rsqrt(jnp.mean(values * values, axis=-1, keepdims=True) + EPSILON)


def unit_back(values, cotangent):
    inverse = lax.rsqrt(jnp.mean(values * values, axis=-1, keepdims=True) + EPSILON)
    along = jnp.mean(cotangent * values, axis=-1, keepdims=True)
    return inverse * cotangent - values * (inverse * inverse * inverse * along)


def image_layout(image_sizes):
    span_ends = jnp.cumsum(image_sizes, dtype=jnp.int32)
    span_starts = span_ends - image_sizes
    places = jnp.arange(MERGED, dtype=jnp.int32)
    image_of = jnp.sum(
        (places[:, None] >= span_ends[None, :]).astype(jnp.int32), axis=1, dtype=jnp.int32
    )
    onehot = image_of[:, None] == jnp.arange(image_sizes.shape[0], dtype=jnp.int32)[None, :]
    offset = jnp.sum(jnp.where(onehot, span_starts[None, :], 0), axis=1, dtype=jnp.int32)
    return (image_of, places - offset, onehot)


def gather_blocks(place_ref, blocks, held, turned):
    for step in range(QUARTERS):
        if turned:
            owner = lax.rem(place_ref[0] - step + QUARTERS, QUARTERS)
            rows = pl.ds(pl.multiple_of(owner * TOKENS, 16), TOKENS)
        else:
            rows = slice(step * TOKENS, (step + 1) * TOKENS)
        held[rows, :] = blocks[step][...]


def head_parts(projected, head):
    at = 3 * HEAD * head
    return (
        projected[:, at : at + HEAD],
        projected[:, at + HEAD : at + 2 * HEAD],
        projected[:, at + 2 * HEAD : at + 3 * HEAD],
    )


def head_weights(queries, keys, same):
    scores = jnp.where(same, dot_nt(queries, keys) * SCALE, -1000000000.0)
    raised = jnp.exp(scores - jnp.max(scores, axis=-1, keepdims=True))
    return raised / jnp.sum(raised, axis=-1, keepdims=True)


def inner_rows(held, weight, same):
    normed = unit_rows(held[...].astype(f32)).astype(bf16)
    projected = dot(normed, weight[:, :QKV]).astype(bf16)
    mixed = []
    for head in range(HEADS):
        queries, keys, values = head_parts(projected, head)
        mixed.append(dot(head_weights(queries, keys, same).astype(bf16), values).astype(bf16))
    return normed, projected, jnp.concatenate(mixed, axis=1)


def forward_kernel(place_ref, down, across_ref, x0, x1, x2, x3, weight, part, held, *, turned):
    gather_blocks(place_ref, (x0, x1, x2, x3), held, turned)
    same = down[...] == across_ref[...]
    _, _, mixed = inner_rows(held, weight, same)
    total = dot_nt(mixed, weight[:, PROJ_AT:]).astype(bf16)
    for quarter in range(QUARTERS):
        part[quarter] = total[quarter * TOKENS : (quarter + 1) * TOKENS]


def keep_kernel(place_ref, down, across_ref, x0, x1, x2, x3, weight, normed, projected, mixed, held):
    gather_blocks(place_ref, (x0, x1, x2, x3), held, True)
    same = down[...] == across_ref[...]
    normed[...], projected[...], mixed[...] = inner_rows(held, weight, same)


def grad_heads(grad_out, projected, weight, same):
    grad_mixed = dot(grad_out, weight[:, PROJ_AT:]).astype(bf16)
    pieces = []
    for head in range(HEADS):
        queries, keys, values = head_parts(projected, head)
        weights = head_weights(queries, keys, same)
        grad_head = grad_mixed[:, HEAD * head : HEAD * (head + 1)]
        grad_values = dot_tn(weights.astype(bf16), grad_head)
        grad_weights = dot_nt(grad_head, values).astype(bf16).astype(f32)
        centre = jnp.sum(grad_weights * weights, axis=-1, keepdims=True)
        grad_scores = (weights * (grad_weights - centre) * SCALE).astype(bf16)
        pieces += [dot(grad_scores, keys), dot_tn(grad_scores, queries), grad_values]
    return jnp.concatenate([piece.astype(bf16) for piece in pieces], axis=1)


def backward_kernel(
    place_ref,
    down,
    across_ref,
    g0,
    g1,
    g2,
    g3,
    projected,
    weight,
    g_before,
    p_before,
    g_after,
    p_after,
    part,
    held,
    *,
    turned,
):
    gather_blocks(place_ref, (g0, g1, g2, g3), held, turned)
    same = down[...] == across_ref[...]
    grad_out = held[...]
    grad_projected = grad_heads(grad_out, projected[...], weight, same)
    total = dot_nt(grad_projected, weight[:, :QKV]).astype(bf16)
    for quarter in range(QUARTERS):
        part[quarter] = total[quarter * TOKENS : (quarter + 1) * TOKENS]
    g_after[...] = g_before[...] + grad_out
    p_after[...] = p_before[...] + grad_projected


def last_kernel(
    place_ref,
    down,
    across_ref,
    g0,
    g1,
    g2,
    g3,
    projected,
    weight,
    g_before,
    p_before,
    normed,
    mixed,
    joint_grad,
    held,
):
    gather_blocks(place_ref, (g0, g1, g2, g3), held, True)
    same = down[...] == across_ref[...]
    grad_projected = p_before[...] + grad_heads(held[...], projected[...], weight, same)
    step = WIDTH // 5
    for at in range(0, WIDTH, step):
        rows = slice(at, at + step)
        joint_grad[rows, :QKV] = dot_tn(normed[:, rows], grad_projected).astype(bf16)
        joint_grad[rows, QKV:PROJ_AT] = jnp.zeros((step, PROJ_AT - QKV), bf16)
        grad_rows = g_before[:, rows] + held[:, rows]
        joint_grad[rows, PROJ_AT:] = dot_tn(grad_rows, mixed[...]).astype(bf16)


def merge_kernel(_, blocks, weight, grad_act, merged, activated, grad_before, part):
    before = jnp.zeros((TOKENS, HIDDEN), f32)
    for quarter in range(QUARTERS):
        at = slice(quarter * WIDTH, (quarter + 1) * WIDTH)
        normed = unit_rows(blocks[quarter].astype(f32)).astype(bf16)
        for part_at in range(4):
            merged[4 * quarter + part_at] = normed[:, HIDDEN * part_at : HIDDEN * (part_at + 1)]
        before = before + dot_nt(normed, weight[:, at])
    tail = 0.5 * (1.0 + lax.erf(before * math.sqrt(0.5)))
    bell = jnp.exp(-0.5 * before * before) * (1.0 / math.sqrt(2.0 * math.pi))
    activated[...] = (before * tail).astype(bf16)
    grad = ((tail + before * bell) * grad_act[...]).astype(bf16)
    grad_before[...] = grad
    for quarter in range(QUARTERS):
        at = slice(quarter * WIDTH, (quarter + 1) * WIDTH)
        part[quarter] = dot(grad, weight[:, at]).astype(bf16)


def merger_grad_kernel(merged, grad_before, activated, visual_grad, out):
    out[0, :, :FEATURES] = dot_tn(activated[...], visual_grad[0]).astype(bf16)
    out[0, :, FEATURES:] = dot_tn(merged[0], grad_before[...]).astype(bf16)


def merger_grads(merged, grad_before, activated, visual_grad):
    whole = pl.BlockSpec((TOKENS, HIDDEN), lambda j: (0, 0))
    return pl.pallas_call(
        merger_grad_kernel,
        grid=(16,),
        in_specs=[
            pl.BlockSpec((1, TOKENS, HIDDEN), lambda j: (j, 0, 0)),
            whole,
            whole,
            pl.BlockSpec((1, TOKENS, FEATURES), lambda j: (j, 0, 0)),
        ],
        out_specs=pl.BlockSpec((1, HIDDEN, FEATURES + HIDDEN), lambda j: (j, 0, 0)),
        out_shape=jax.ShapeDtypeStruct((16, HIDDEN, FEATURES + HIDDEN), bf16),
        compiler_params=pltpu.CompilerParams(vmem_limit_bytes=16 * 1024 * 1024),
        cost_estimate=pl.CostEstimate(
            flops=2 * TOKENS * 16 * HIDDEN * (FEATURES + HIDDEN),
            bytes_accessed=4 * 16 * HIDDEN * (FEATURES + HIDDEN),
            transcendentals=0,
        ),
    )(merged, grad_before, activated, visual_grad)


def call(kernel, operands, results, scratch, flops, moved):
    return pl.pallas_call(
        kernel,
        in_specs=[pl.BlockSpec(memory_space=pltpu.SMEM)]
        + [pl.BlockSpec(memory_space=pltpu.VMEM)] * (len(operands) - 1),
        out_specs=[pl.BlockSpec(memory_space=pltpu.VMEM)] * len(results),
        out_shape=[jax.ShapeDtypeStruct(shape, kind) for shape, kind in results],
        scratch_shapes=[pltpu.VMEM(shape, kind) for shape, kind in scratch],
        compiler_params=pltpu.CompilerParams(vmem_limit_bytes=40 * 1024 * 1024),
        cost_estimate=pl.CostEstimate(flops=flops, bytes_accessed=moved, transcendentals=0),
    )(*operands)


PART = ((QUARTERS, TOKENS, WIDTH), bf16)


def local(
    patches,
    image_sizes,
    raster_order,
    image_starts,
    qkv_weight,
    proj_weight,
    merge_in,
    merge_out,
    text_embeds,
    joined_grad,
):
    section = lax.axis_index("section")
    place = lax.axis_index("mp")
    place_ref = place.reshape(1)
    is_last = section == SECTIONS - 1

    joint_local = jnp.concatenate(
        [qkv_weight[0], jnp.zeros((WIDTH // 16, PROJ_AT - QKV), bf16), proj_weight[0].T], axis=1
    )
    joint = lax.all_gather(joint_local, "dp", axis=0, tiled=True)

    marks = []
    spots = []
    for micro in range(2):
        image_of, within, onehot = image_layout(image_sizes[micro, 0])
        window_of = image_of * MERGED + within // WINDOW
        marks.append(jnp.where(is_last, image_of, window_of) + micro * 1024)
        starts = jnp.where(onehot, image_starts[micro, 0][None, :], 0)
        slots = jnp.sum(starts, axis=1, dtype=jnp.int32) + within
        order = raster_order[micro]
        from_raster = order[None, :] == jnp.arange(MERGED, dtype=jnp.int32)[:, None]
        spots.append(jnp.sum(jnp.where(from_raster, slots[None, :], 0), axis=1, dtype=jnp.int32))
    mark = jnp.tile(jnp.concatenate(marks), QUARTERS)
    down, right = mark[:, None], mark[None, :]
    positions = jnp.arange(text_embeds.shape[1], dtype=jnp.int32)
    chosen = jnp.stack(spots)[:, :, None] == positions[None, None, :]
    chosen_bf = chosen.astype(bf16)

    visual_grad = jnp.einsum(
        "mts,msf->mtf", chosen_bf, joined_grad, preferred_element_type=f32
    ).astype(bf16)
    visual_grad = visual_grad.reshape(TOKENS, FEATURES)
    visual_grad_full = lax.all_gather(visual_grad, ("section", "mp"), axis=0)
    grad_act = jnp.einsum(
        "jtf,rjf->tr",
        visual_grad_full,
        merge_out.reshape(HIDDEN, 16, FEATURES),
        preferred_element_type=f32,
    )

    quarters = jnp.swapaxes(patches.reshape(TOKENS, QUARTERS, WIDTH), 0, 1)
    quarters, visual_grad_full, grad_act = lax.optimization_barrier(
        (quarters, visual_grad_full, grad_act)
    )
    first = section == 0
    blocks = [quarters[quarter] for quarter in range(QUARTERS)]
    own = lax.dynamic_index_in_dim(quarters, place, 0, False)
    saved = [
        lax.dynamic_index_in_dim(quarters, (place + QUARTERS - step) % QUARTERS, 0, False)
        for step in range(QUARTERS)
    ]
    saved = [jnp.where(first, block, jnp.zeros_like(block)) for block in saved]

    layer_flops = 2 * ROWS * WIDTH * JOINT
    layer_bytes = 2 * WIDTH * JOINT + 8 * ROWS * WIDTH
    held = ((ROWS, WIDTH), bf16)
    for stage in range(SECTIONS):
        (terms,) = call(
            functools.partial(forward_kernel, turned=stage > 0),
            [place_ref, down, right, *blocks, joint],
            [PART],
            [held],
            layer_flops,
            layer_bytes,
        )
        total = own.astype(f32) + jnp.sum(exchange(terms).astype(f32), axis=0)
        own = total.astype(bf16)
        if stage < SECTIONS - 1:
            blocks = to_section(own, stage, stage + 1)
            saved = [old + new for old, new in zip(saved, blocks)]
            own = blocks[0]

    sent = [permute(own, across(SECTIONS - 1, target)) for target in range(SECTIONS - 1)]
    own = jnp.where(is_last, own, sent[0] + sent[1] + sent[2])
    merged, activated, grad_before, terms = call(
        merge_kernel,
        [place_ref, everyones(own), merge_in.T, grad_act],
        [
            ((16, TOKENS, HIDDEN), bf16),
            ((TOKENS, HIDDEN), bf16),
            ((TOKENS, HIDDEN), bf16),
            PART,
        ],
        [],
        4 * TOKENS * QUARTERS * WIDTH * HIDDEN,
        2 * QUARTERS * WIDTH * HIDDEN,
    )
    normed, projected, mixed = call(
        keep_kernel,
        [place_ref, down, right, *saved, joint],
        [((ROWS, WIDTH), bf16), ((ROWS, QKV), bf16), ((ROWS, MIX), bf16)],
        [held],
        layer_flops,
        layer_bytes,
    )

    total = jnp.sum(exchange(terms).astype(f32), axis=0)
    leaving = total.astype(bf16)
    leaving, merged, normed = lax.optimization_barrier((leaving, merged, normed))
    arrived = [permute(leaving, across(s, SECTIONS - 1)) for s in range(SECTIONS - 1)]
    merger_grad = merger_grads(merged, grad_before, activated, visual_grad_full)
    *arrived, merger_grad = lax.optimization_barrier((*arrived, merger_grad))
    merger_grad = lax.psum_scatter(merger_grad, "dp", scatter_dimension=0, tiled=False)
    total = leaving.astype(f32)
    for term in arrived:
        total = total + term.astype(f32)
    grad_own = unit_back(own.astype(f32), total)
    grad_own = jnp.where(is_last, grad_own, 0.0).astype(bf16)

    grad_rows = jnp.zeros((ROWS, WIDTH), bf16)
    grad_projected = jnp.zeros((ROWS, QKV), bf16)
    gathered = everyones(grad_own)
    grads = [gathered[quarter] for quarter in range(QUARTERS)]
    for layer in range(SECTIONS - 1, 0, -1):
        grad_rows, grad_projected, terms = call(
            functools.partial(backward_kernel, turned=layer < SECTIONS - 1),
            [place_ref, down, right, *grads, projected, joint, grad_rows, grad_projected],
            [((ROWS, WIDTH), bf16), ((ROWS, QKV), bf16), PART],
            [held],
            layer_flops,
            layer_bytes,
        )
        total = jnp.sum(exchange(terms).astype(f32), axis=0)
        grad_own = grad_own.astype(f32) + unit_back(saved[0].astype(f32), total)
        grad_own = grad_own.astype(bf16)
        grads = to_section(grad_own, layer, layer - 1)
        grad_own = grads[0]
    (joint_grad,) = call(
        last_kernel,
        [
            place_ref,
            down,
            right,
            *grads,
            projected,
            joint,
            grad_rows,
            grad_projected,
            normed,
            mixed,
        ],
        [((WIDTH, JOINT), bf16)],
        [held],
        2 * layer_flops,
        2 * layer_bytes,
    )
    joint_grad, merger_grad = lax.optimization_barrier((joint_grad, merger_grad))
    reduced = lax.psum_scatter(joint_grad, "dp", scatter_dimension=0, tiled=True)
    qkv_grad = reduced[:, :QKV].astype(f32)
    proj_grad = reduced[:, PROJ_AT:].T.astype(f32)

    activated, joint_grad = lax.optimization_barrier((activated, joint_grad))
    visual_terms = jnp.einsum(
        "tr,rjf->jtf",
        activated,
        merge_out.reshape(HIDDEN, 16, FEATURES),
        preferred_element_type=f32,
    ).astype(bf16)
    visual = lax.all_to_all(visual_terms, ("section", "mp"), 0, 0)
    visual = jnp.sum(visual.astype(f32), axis=0).astype(bf16).reshape(2, MERGED, FEATURES)
    placed = jnp.einsum("mts,mtf->msf", chosen_bf, visual, preferred_element_type=f32)
    taken = jnp.any(chosen, axis=1)[:, :, None]
    joined = jnp.where(taken, placed.astype(bf16), text_embeds)
    merge_out_grad = merger_grad[:, :FEATURES].astype(f32)
    merge_in_grad = merger_grad[:, FEATURES:].astype(f32)
    return (joined, qkv_grad[None], proj_grad[None], merge_in_grad, merge_out_grad)


def solution(mesh):
    return jax.shard_map(
        local,
        mesh=mesh,
        in_specs=(
            P(None, "dp", None),
            P(None, "dp", None),
            P(None, "dp"),
            P(None, "dp", None),
            P("section", "dp", "mp"),
            P("section", "mp", "dp"),
            P(None, ("section", "mp")),
            P(("section", "mp"), None),
            P(None, "dp", ("section", "mp")),
            P(None, "dp", ("section", "mp")),
        ),
        out_specs=(
            P(None, "dp", ("section", "mp")),
            P("section", "dp", "mp"),
            P("section", "mp", "dp"),
            P("dp", ("section", "mp")),
            P(("section", "mp"), "dp"),
        ),
        check_vma=False,
    )
```
